32 devices in a mesh: dp: 8 (over y, x, core), tensor: 4 (over z).
Axes of the slice: x: 2, y: 2, z: 4, core: 2. Of those that a mesh axis runs over, the one named last changes fastest.
Arguments:
- block_in: bfloat16 [8, 1024, 1024], P('dp', 'tensor'), may hold values from -6 to 6
- segment_ids: int32 [8, 1024], P('dp', 'tensor'), may hold values from 0 to 2, as said below
- norm1_gain: float32 [1024], replicated, may hold values from 0.1 to 1.9
- w_qkv: bfloat16 [3, 1024, 1024], P(None, 'dp', 'tensor'), may hold values from -0.1875 to 0.1875
- w_out: bfloat16 [1024, 1024], P('tensor', 'dp'), may hold values from -3 to 3
- norm2_gain: float32 [1024], replicated, may hold values from 0.1 to 1.9
- w_in: bfloat16 [2, 1024, 2624], P(None, 'dp', 'tensor'), may hold values from -0.1875 to 0.1875
- w_mlp_out: bfloat16 [2624, 1024], P('tensor', 'dp'), may hold values from -0.125 to 0.125
- out_grad: bfloat16 [8, 1024, 1024], P('dp', 'tensor'), may hold values from -6 to 6
Outputs:
- block_out: bfloat16 [8, 1024, 1024], P('dp', 'tensor')
- in_grad: float32 [8, 1024, 1024], P('dp', 'tensor')
- norm1_grad: float32 [1024], replicated
- w_qkv_grad: float32 [3, 1024, 1024], P(None, 'dp', 'tensor')
- w_out_grad: float32 [1024, 1024], P('tensor', 'dp')
- norm2_grad: float32 [1024], replicated
- w_in_grad: float32 [2, 1024, 2624], P(None, 'dp', 'tensor')
- w_mlp_out_grad: float32 [2624, 1024], P('tensor', 'dp')
The draws below stay inside these ranges and needn't reach their ends.
Inputs may be any that keep to these rules, and one draw needn't show every extreme that they name: `segment_ids`: ids never fall along a sequence; each sequence holds three documents, the first starting at position 0 and the last ending at position 1023, both shorter than 256 tokens.
All inputs are finite; a program needn't handle non-finite values.
Results may differ from the reference program's by a relative error of at most 0.017.
Values may be sent and summed in bfloat16 or wider, within the bound.
No kernel may reach another device: no remote copies, remote signals or barrier semaphores. Data moves between devices by JAX's collectives and lax.ppermute only.
A program may use at most 128 MiB of HBM per device.

```python
import jax
import jax.numpy as jnp
from jax import lax

D = 1024
HEAD_DIM = 64
FF = 2624
LENGTH = 1024
SEQS = 8
PIECE = 256


def draw_segment_ids(key, part):
    key = jax.random.fold_in(key, 11)
    head_key, tail_key = jax.random.split(key)
    head_len = jax.random.randint(head_key, (SEQS, 1), 1, PIECE)
    tail_len = jax.random.randint(tail_key, (SEQS, 1), 1, PIECE)
    places = jnp.arange(LENGTH, dtype=jnp.int32)[None, :]
    return (places >= head_len).astype(jnp.int32) + (places >= LENGTH - tail_len).astype(jnp.int32)


def spiked(entries, stream_key, source, target, shards_of, factor):
    def block_of(position):
        return (jnp.arange(entries.shape[position]) // (entries.shape[position] // shards_of)).reshape((-1,) + (1,) * (entries.ndim - 1 - position))

    one_side = jax.random.permutation(stream_key, shards_of)[block_of(target)]
    second = (block_of(target) + shards_of // 2) % shards_of
    return jnp.where((block_of(source) == one_side) | (block_of(source) == second), factor * entries, entries)


def levels(rng, shape, shards, least, largest):
    factor_of = 1.0
    for axis_at, blocks in shards:
        steps = jax.random.uniform(jax.random.fold_in(jax.random.fold_in(rng, 6), axis_at), (blocks,), jnp.float32, least / len(shards), largest / len(shards))
        factor_of = factor_of * jnp.repeat(jnp.exp(steps), shape[axis_at] // blocks).reshape((-1,) + (1,) * (len(shape) - 1 - axis_at))
    return factor_of


def gaussian(stream_key, shape, width, bound, cuts=(), kind=jnp.bfloat16):
    loudness = levels(stream_key, shape, cuts, -0.22, 0.18) if cuts else 1.0
    entries = jax.random.normal(stream_key, shape, jnp.float32) * width * loudness
    return jnp.minimum(jnp.maximum(entries, -bound), bound).astype(kind)


def gaussian_with(own_key, dims, scale, bound, cuts, heavy, kind=jnp.bfloat16):
    result = scale * jax.random.normal(own_key, dims, jnp.float32)
    if cuts:
        result = result * levels(own_key, dims, cuts, -0.22, 0.18)
    return jnp.clip(spiked(result, jax.random.fold_in(own_key, 3), *heavy), -bound, bound).astype(kind)


def setup_inputs(seed: int = 0) -> dict:
    arg_keys = jax.random.split(jax.random.key(seed), 10)
    block_in = gaussian(arg_keys[0], (SEQS, LENGTH, D), 1.0, 6.0, ((0, 8), (1, 4)))
    segment_ids = draw_segment_ids(jax.random.fold_in(arg_keys[9], 71), 0)
    norm1_gain = jnp.clip(1.0 + 0.18 * jax.random.normal(arg_keys[2], (D,), jnp.float32), 0.1, 1.9)
    w_qkv = gaussian(arg_keys[3], (3, D, D), D ** -0.5, 0.1875, ((1, 8), (2, 4)))
    w_out = gaussian(arg_keys[4], (D, D), (max(D // 256, 1)) ** -0.5, 3.0, ((0, 4), (1, 8)))
    norm2_gain = jnp.clip(1.0 + 0.18 * jax.random.normal(arg_keys[5], (D,), jnp.float32), 0.1, 1.9)
    w_in = gaussian(arg_keys[6], (2, D, FF), D ** -0.5, 0.1875, ((1, 8), (2, 4)))
    w_mlp_out = gaussian(arg_keys[7], (FF, D), FF ** -0.5, 0.125, ((0, 4), (1, 8)))
    out_grad = gaussian_with(arg_keys[8], (SEQS, LENGTH, D), 1.0, 6.0, ((0, 8), (1, 4)), (0, 2, 8, 2.0))
    return dict(block_in=block_in, segment_ids=segment_ids, norm1_gain=norm1_gain, w_qkv=w_qkv, w_out=w_out, norm2_gain=norm2_gain, w_in=w_in, w_mlp_out=w_mlp_out, out_grad=out_grad)


EPSILON = 1e-05
ROPE_BASE = 160000.0
MASKED = -1e+30
HIGHEST = lax.Precision.HIGHEST

@jax.custom_vjp
def low(v):
    return lax.optimization_barrier(v.astype(jnp.bfloat16)).astype(jnp.float32)

@jax.custom_vjp
def low_back(v):
    return v

def low_keep(v):
    return (low(v), None)

def low_pass(kept, grad):
    return (grad,)

def back_keep(v):
    return (v, None)

def back_low(kept, grad):
    return (low(grad),)
low.defvjp(low_keep, low_pass)
low_back.defvjp(back_keep, back_low)

def layer_norm(inputs, gain):
    average = lax.optimization_barrier(jnp.mean(inputs, axis=-1, keepdims=True))
    centred = inputs - average
    variance = lax.optimization_barrier(jnp.mean(centred * centred, axis=-1, keepdims=True))
    return centred * lax.rsqrt(variance + EPSILON) * gain

def positions_of(segments):
    places = jnp.arange(segments.shape[0], dtype=jnp.int32)
    starts = jnp.concatenate([jnp.ones((1,), jnp.bool_), segments[1:] != segments[:-1]])
    first = lax.cummax(jnp.where(starts, places, jnp.zeros_like(places)), axis=0)
    return places - first

def rotary_tables(segments):
    half_dim = HEAD_DIM // 2
    freqs = jnp.power(ROPE_BASE, -jnp.arange(half_dim, dtype=jnp.float32) * 2.0 / HEAD_DIM)
    angles = positions_of(segments).astype(jnp.float32)[:, None] * freqs[None, :]
    return (jnp.cos(angles)[:, None, :], jnp.sin(angles)[:, None, :])

def rotate(inputs, cosine, sine):
    half_dim = inputs.shape[-1] // 2
    first, second = (inputs[..., :half_dim], inputs[..., half_dim:])
    return jnp.concatenate([first * cosine - second * sine, second * cosine + first * sine], axis=-1)

def attend_block(query_block, seg_block, key_rows, value_rows, segments):
    raw = jnp.einsum('qhd,khd->hqk', query_block, key_rows, precision=HIGHEST) * HEAD_DIM ** (-0.5)
    scores = low_back(raw)
    same = (seg_block[:, None] == segments[None, :])[None]
    scores = jnp.where(same, scores, MASKED)
    highest = lax.optimization_barrier(jnp.max(scores, axis=-1, keepdims=True))
    weights = jnp.exp(scores - highest)
    chances = low(weights / lax.optimization_barrier(jnp.sum(weights, axis=-1, keepdims=True)))
    return jnp.einsum('hqk,khd->qhd', chances, value_rows, precision=HIGHEST)

def one_sequence(inputs, segments, gain1, qkv, proj, gain2, expand, contract):
    length = inputs.shape[0]
    heads = qkv.shape[2] // HEAD_DIM
    normed = low(layer_norm(inputs, gain1))
    query_rows = low_back(jnp.dot(normed, qkv[0], precision=HIGHEST))
    key_rows = low_back(jnp.dot(normed, qkv[1], precision=HIGHEST))
    value_rows = low(low_back(jnp.dot(normed, qkv[2], precision=HIGHEST)))
    cosine, sine = rotary_tables(segments)
    query_rows = low(rotate(query_rows.reshape(length, heads, HEAD_DIM), cosine, sine))
    key_rows = low(rotate(key_rows.reshape(length, heads, HEAD_DIM), cosine, sine))
    value_rows = value_rows.reshape(length, heads, HEAD_DIM)
    block_rows = min(512, length)
    query_blocks = query_rows.reshape(length // block_rows, block_rows, heads, HEAD_DIM)
    seg_blocks = segments.reshape(length // block_rows, block_rows)
    checked = jax.checkpoint(attend_block)
    mixed = lax.map(lambda operands: checked(operands[0], operands[1], key_rows, value_rows, segments), (query_blocks, seg_blocks))
    context = low(low_back(mixed.reshape(length, heads * HEAD_DIM)))
    branch = low_back(jnp.dot(context, proj, precision=HIGHEST))
    hidden = inputs + branch
    normed2 = low(layer_norm(hidden, gain2))
    act_in = low_back(jnp.dot(normed2, expand[0], precision=HIGHEST))
    gate_in = low_back(jnp.dot(normed2, expand[1], precision=HIGHEST))
    product = low(jax.nn.gelu(act_in, approximate=False) * gate_in)
    mlp_branch = low_back(jnp.dot(product, contract, precision=HIGHEST))
    return hidden + mlp_branch

def reference(block_in, segment_ids, norm1_gain, w_qkv, w_out, norm2_gain, w_in, w_mlp_out, out_grad):

    def forward(inputs, gain1, qkv, proj, gain2, expand, contract):
        return lax.map(lambda operands: one_sequence(operands[0], operands[1], gain1, qkv, proj, gain2, expand, contract), (inputs, segment_ids))
    primals = (block_in.astype(jnp.float32), norm1_gain.astype(jnp.float32), w_qkv.astype(jnp.float32), w_out.astype(jnp.float32), norm2_gain.astype(jnp.float32), w_in.astype(jnp.float32), w_mlp_out.astype(jnp.float32))
    outputs, pullback = jax.vjp(forward, *primals)
    grad_input, grad_gain1, grad_qkv, grad_proj, grad_gain2, grad_expand, grad_contract = pullback(out_grad.astype(jnp.float32))
    return (outputs.astype(jnp.bfloat16), grad_input, grad_gain1, grad_qkv, grad_proj, grad_gain2, grad_expand, grad_contract)
```

```python
import functools

import jax
import jax.numpy as jnp
from jax import lax
from jax.experimental import pallas as pl
from jax.experimental.pallas import tpu as pltpu
from jax.sharding import PartitionSpec as P

HEAD_DIM = 64
HALF = HEAD_DIM // 2
EPSILON = 1e-05
ROPE_BASE = 160000.0
MASKED = -1e30
ROWS = 256
SCALE = HEAD_DIM ** (-0.5)
F32 = jnp.float32
BF16 = jnp.bfloat16


def dot(a, b, dims):
    return lax.dot_general(a, b, ((dims[0], dims[1]), ((), ())), preferred_element_type=F32)


NN = ((1,), (0,))
NT = ((1,), (1,))
TN = ((0,), (0,))


def spin(u, cosine, sine):
    width = u.shape[-1]
    lane = lax.broadcasted_iota(jnp.int32, u.shape, 1)
    other = jnp.where(
        lane % HEAD_DIM < HALF, pltpu.roll(u, width - HALF, 1), pltpu.roll(u, HALF, 1)
    )
    return u * cosine + other * sine


def head_mask(shape, head):
    lane = lax.broadcasted_iota(jnp.int32, shape, 1)
    return lane // HEAD_DIM == head


def attend_kernel(rows, normed, w_qkv, cosine, sine, seg_col, seg_row, q, k, v, ctx, lse):
    length, width = q.shape
    heads = width // HEAD_DIM

    @pl.loop(0, length // rows)
    def _(block):
        here = pl.ds(pl.multiple_of(block * rows, rows), rows)
        proj = dot(normed[here, :], w_qkv[...], NN)
        cos_here, sin_here = cosine[here, :], sine[here, :]
        q[here, :] = spin(proj[:, :width], cos_here, sin_here).astype(BF16)
        k[here, :] = spin(proj[:, width : 2 * width], cos_here, sin_here).astype(BF16)
        v[here, :] = proj[:, 2 * width :].astype(BF16)

    @pl.loop(0, length // rows)
    def _(block):
        here = pl.ds(pl.multiple_of(block * rows, rows), rows)
        q_here = q[here, :]
        same = seg_col[here, :] == seg_row[...]
        total = jnp.zeros((rows, width), F32)
        for head in range(heads):
            mine = head_mask((rows, width), head)
            q_head = jnp.where(mine, q_here, jnp.zeros_like(q_here)) * BF16(SCALE)
            scores = jnp.where(same, dot(q_head, k[...], NT), MASKED)
            highest = jnp.max(scores, axis=1, keepdims=True)
            weights = jnp.exp(scores - highest)
            sums = jnp.sum(weights, axis=1, keepdims=True)
            mixed = dot(weights.astype(BF16), v[...], NN) * (1.0 / sums)
            total = jnp.where(mine, mixed, total)
            lse[here, head : head + 1] = highest + jnp.log(sums)
        ctx[here, :] = total.astype(BF16)


def attend(normed, w_qkv, cosine, sine, seg_col, seg_row):
    length = normed.shape[0]
    width = w_qkv.shape[1] // 3
    rows = min(ROWS, length)
    heads = width // HEAD_DIM
    cost = pl.CostEstimate(
        flops=2 * length * normed.shape[1] * 3 * width + 4 * length * length * width * 4,
        bytes_accessed=8 * 2**20,
        transcendentals=heads * length * length,
    )
    wide = jax.ShapeDtypeStruct((length, width), BF16)
    return pl.pallas_call(
        functools.partial(attend_kernel, rows),
        out_shape=(wide, wide, wide, wide, jax.ShapeDtypeStruct((length, 128), F32)),
        compiler_params=pltpu.CompilerParams(vmem_limit_bytes=48 * 2**20),
        cost_estimate=cost,
        name="attend",
    )(normed, w_qkv, cosine, sine, seg_col, seg_row)


def attend_back_kernel(
    rows, dctx, q, k, v, lse_row, cosine, sine, seg_col, seg_row, dproj, dk_sum, dv_sum
):
    length, width = q.shape
    heads = width // HEAD_DIM
    dk_sum[...] = jnp.zeros_like(dk_sum)
    dv_sum[...] = jnp.zeros_like(dv_sum)

    @pl.loop(0, length // rows)
    def _(block):
        here = pl.ds(pl.multiple_of(block * rows, rows), rows)
        q_here, dctx_here = q[here, :], dctx[here, :]
        same = seg_col[...] == seg_row[:, here]
        dq = jnp.zeros((rows, width), F32)
        for head in range(heads):
            mine = head_mask((rows, width), head)
            q_head = jnp.where(mine, q_here, jnp.zeros_like(q_here)) * BF16(SCALE)
            dctx_head = jnp.where(mine, dctx_here, jnp.zeros_like(dctx_here))
            scores = jnp.where(same, dot(k[...], q_head, NT), MASKED)
            chances = jnp.exp(scores - lse_row[head : head + 1, here])
            grads = dot(v[...], dctx_head, NT)
            both = chances * grads
            inner = jnp.sum(both, axis=0, keepdims=True)
            dscores = (both - chances * inner).astype(BF16)
            dv_sum[...] += dot(chances.astype(BF16), dctx_head, NN)
            dk_sum[...] += dot(dscores, q_head, NN)
            dq = jnp.where(mine, dot(dscores, k[...], TN), dq)
        dq = spin(dq * SCALE, cosine[here, :], -sine[here, :])
        dproj[here, :width] = dq.astype(BF16)

    @pl.loop(0, length // rows)
    def _(block):
        here = pl.ds(pl.multiple_of(block * rows, rows), rows)
        dk = spin(dk_sum[here, :], cosine[here, :], -sine[here, :])
        dproj[here, width : 2 * width] = dk.astype(BF16)
        dproj[here, 2 * width :] = dv_sum[here, :].astype(BF16)


def attend_back(dctx, q, k, v, lse_row, cosine, sine, seg_col, seg_row):
    length, width = q.shape
    rows = min(ROWS, length)
    heads = width // HEAD_DIM
    cost = pl.CostEstimate(
        flops=10 * length * length * width * 4,
        bytes_accessed=8 * 2**20,
        transcendentals=heads * length * length,
    )
    return pl.pallas_call(
        functools.partial(attend_back_kernel, rows),
        out_shape=jax.ShapeDtypeStruct((length, 3 * width), BF16),
        scratch_shapes=[pltpu.VMEM((length, width), F32), pltpu.VMEM((length, width), F32)],
        compiler_params=pltpu.CompilerParams(vmem_limit_bytes=48 * 2**20),
        cost_estimate=cost,
        name="attend_back",
    )(dctx, q, k, v, lse_row, cosine, sine, seg_col, seg_row)


def normalize(rows):
    average = jnp.mean(rows, axis=-1, keepdims=True)
    centred = rows - average
    inv_std = lax.rsqrt(jnp.mean(centred * centred, axis=-1, keepdims=True) + EPSILON)
    return centred * inv_std, inv_std


def norm_back(grads, gain, scaled, inv_std):
    inner = grads * gain
    mean_grad = jnp.mean(inner, axis=-1, keepdims=True)
    mean_proj = jnp.mean(inner * scaled, axis=-1, keepdims=True)
    return inv_std * (inner - mean_grad - scaled * mean_proj)


def on_device(
    n_dp,
    n_t,
    block_in,
    segment_ids,
    norm1_gain,
    w_qkv,
    w_out,
    norm2_gain,
    w_in,
    w_mlp_out,
    out_grad,
):
    n_quad = n_dp // 2
    bits = [1 << b for b in range(n_quad.bit_length() - 1)]
    d_index, t_index = lax.axis_index("dp"), lax.axis_index("tensor")
    quad, first_core = d_index // 2, d_index % 2 == 0
    piece, d_model = block_in.shape[1], block_in.shape[2]
    length = piece * n_t
    width = w_qkv.shape[2]
    span = d_model // n_quad

    def core(x):
        return lax.ppermute(x, "dp", [(i, i ^ 1) for i in range(n_dp)])

    def pair(x, bit):
        return lax.ppermute(x, "dp", [(i, i ^ (2 * bit)) for i in range(n_dp)])

    def ahead(x, by):
        return lax.ppermute(x, "tensor", [(i, (i + by) % n_t) for i in range(n_t)])

    def across(x, mask):
        return lax.ppermute(x, "tensor", [(i, i ^ mask) for i in range(n_t)])

    def pick(a, b):
        return jnp.where(first_core, a, b)

    def reorder(x):
        cuts = [
            lax.dynamic_slice_in_dim(x, (quad ^ m) * span, span, axis=x.ndim - 1)
            for m in range(n_quad)
        ]
        return jnp.concatenate(cuts, axis=-1)

    def pair_gather(x, order):
        held = {0: x}
        for bit in order:
            held.update({m ^ bit: pair(block, bit) for m, block in list(held.items())})
        return [held[m] for m in range(n_quad)]

    def pair_scatter(blocks, order):
        held = dict(enumerate(blocks))
        for bit in order:
            held = {
                m: (held[m].astype(F32) + pair(held[m | bit], bit).astype(F32)).astype(BF16)
                for m in held
                if not m & bit
            }
        return held[0]

    def line_gather(x):
        return [x] + [ahead(x, -by) for by in range(1, n_t)]

    x = reorder(block_in[0]).astype(F32)
    gain1, gain2 = reorder(norm1_gain), reorder(norm2_gain)
    scaled1, inv_std1 = normalize(x)
    normed = jnp.concatenate(line_gather((scaled1 * gain1).astype(BF16)), axis=0)
    segments = jnp.concatenate(line_gather(segment_ids), axis=1)

    qkv_local = jnp.concatenate([w_qkv[0], w_qkv[1], w_qkv[2]], axis=1)
    qkv_mine = pair_gather(qkv_local, bits)
    qkv_other = [core(block) for block in qkv_mine]
    qkv_full = jnp.concatenate(
        [
            part
            for mine, other in zip(qkv_mine, qkv_other)
            for part in (pick(mine, other), pick(other, mine))
        ],
        axis=0,
    )
    out_mine = pair_gather(jnp.concatenate(line_gather(w_out), axis=0), bits)
    out_other = [core(block) for block in out_mine]
    out_full = jnp.concatenate(
        [
            part
            for mine, other in zip(out_mine, out_other)
            for part in (pick(mine, other), pick(other, mine))
        ],
        axis=1,
    )

    mlp_local = jnp.stack([w_in[0].T, w_in[1].T, w_mlp_out])
    slices = [mlp_local] + [across(mlp_local, mask) for mask in range(1, n_t)]
    chunks = []
    for j in range(n_t // 2):
        even, odd = slices[2 * j], slices[2 * j + 1]
        other = core(pick(odd, even))
        low = pair_gather(pick(even, other), bits[::-1])
        high = pair_gather(pick(other, odd), bits)
        chunks.append(
            jnp.concatenate([part for both in zip(low, high) for part in both], axis=-1)
        )

    places = (t_index * piece + jnp.arange(length, dtype=jnp.int32)) % length
    firsts = jnp.sum((segments < segments.reshape(length, 1)).astype(jnp.int32), axis=1)
    freqs = jnp.power(ROPE_BASE, -jnp.arange(HALF, dtype=F32) * 2.0 / HEAD_DIM)
    angles = (places - firsts).astype(F32)[:, None] * freqs[None, :]
    cosine, sine = jnp.cos(angles), jnp.sin(angles)
    cosine = jnp.tile(cosine, (1, width // HALF))
    sine = jnp.tile(jnp.concatenate([-sine, sine], axis=1), (1, width // HEAD_DIM))
    seg_col = segments.reshape(length, 1)
    q, k, v, ctx_local, lse = attend(normed, qkv_full, cosine, sine, seg_col, segments)
    lse_row = lse[:, : max(8, width // HEAD_DIM)].T

    ctx_pieces = [ctx_local[:piece]] + [
        ahead(ctx_local[s * piece : (s + 1) * piece], s) for s in range(1, n_t)
    ]
    ctx = jnp.concatenate([ctx_pieces[(n_t - s) % n_t] for s in range(n_t)], axis=1)
    hidden = x + dot(ctx, out_full, NN)

    scaled2, inv_std2 = normalize(hidden)
    normed2 = (scaled2 * gain2).astype(BF16)
    dy = reorder(out_grad[0])
    normed2_both = jnp.concatenate([normed2, core(normed2)], axis=0)
    dy_both = jnp.concatenate([dy, core(dy)], axis=0)
    mlp, dn2 = 0.0, 0.0
    mlp_grads = []
    for up, gate_up, down in chunks:
        act, gate = dot(normed2_both, up, NT), dot(normed2_both, gate_up, NT)
        dprod = dot(dy_both, down, NT)
        below = 0.5 * (1.0 + lax.erf(act * (0.5**0.5)))
        slope = below + act * jnp.exp(-0.5 * act * act) * 0.3989422804014327
        gelu = act * below
        prod = (gelu * gate).astype(BF16)
        dact = (dprod * gate * slope).astype(BF16)
        dgate = (dprod * gelu).astype(BF16)
        mlp += dot(prod, down, NN)
        dn2 += dot(dact, up, NN) + dot(dgate, gate_up, NN)
        mlp_grads.append(
            jnp.stack(
                [
                    dot(dact, normed2_both, TN).astype(BF16),
                    dot(dgate, normed2_both, TN).astype(BF16),
                    dot(prod, dy_both, TN).astype(BF16),
                ]
            )
        )
    mlp_own = mlp[:piece] + core(mlp[piece:].astype(BF16)).astype(F32)
    block_out = reorder((hidden + mlp_own).astype(BF16))
    dn2_own = dn2[:piece] + core(dn2[piece:].astype(BF16)).astype(F32)

    dh = dy.astype(F32) + norm_back(dn2_own, gain2, scaled2, inv_std2)
    gain2_part = jnp.sum(dn2_own * scaled2, axis=0)
    dh_low = dh.astype(BF16)

    dctx = dot(dh_low, out_full, NT).astype(BF16)
    dctx_pieces = [dctx[:, :width]] + [
        ahead(dctx[:, s * width : (s + 1) * width], s) for s in range(1, n_t)
    ]
    dctx_local = jnp.concatenate([dctx_pieces[(n_t - s) % n_t] for s in range(n_t)], axis=0)
    dproj = attend_back(dctx_local, q, k, v, lse_row, cosine, sine, seg_col, segments)
    dn1 = dot(dproj, qkv_full, NT)
    gain1_part = jnp.sum(dn1 * normed.astype(F32), axis=0) / gain1
    dn1_low = dn1.astype(BF16)
    dn1_own = dn1[:piece]
    for s in range(1, n_t):
        dn1_own = dn1_own + ahead(dn1_low[s * piece : (s + 1) * piece], s).astype(F32)
    in_grad = reorder(dh + norm_back(dn1_own, gain1, scaled1, inv_std1))

    block = d_model // n_dp
    ends = []
    for grads in mlp_grads:
        cuts = [grads[:, :, i * block : (i + 1) * block] for i in range(n_dp)]
        low = pair_scatter(cuts[0::2], bits)
        high = pair_scatter(cuts[1::2], bits[::-1])
        kept, other = pick(low, high), core(pick(high, low))
        ends += [pick(kept, other), pick(other, kept)]
    mlp_sum = ends[0].astype(F32)
    for mask in range(1, n_t):
        mlp_sum = mlp_sum + across(ends[mask], mask).astype(F32)
    w_in_grad = jnp.stack([mlp_sum[0].T, mlp_sum[1].T])

    def core_scatter(blocks):
        return [
            (pick(a, b).astype(F32) + core(pick(b, a)).astype(F32)).astype(BF16)
            for a, b in zip(blocks[0::2], blocks[1::2])
        ]

    out_partial = dot(ctx, dh_low, TN).astype(BF16)
    out_cuts = [out_partial[:, i * block : (i + 1) * block] for i in range(n_dp)]
    out_low = pair_scatter(core_scatter(out_cuts), bits)
    out_sum = out_low[:width].astype(F32)
    for s in range(1, n_t):
        out_sum = out_sum + ahead(out_low[s * width : (s + 1) * width], s).astype(F32)

    qkv_partial = dot(normed, dproj, TN).astype(BF16)
    qkv_cuts = [qkv_partial[i * block : (i + 1) * block] for i in range(n_dp)]
    qkv_sum = pair_scatter(core_scatter(qkv_cuts), bits).astype(F32)
    w_qkv_grad = jnp.stack([qkv_sum[:, c * width : (c + 1) * width] for c in range(3)])

    gains = reorder(jnp.stack([gain1_part, gain2_part]))
    gains = gains + core(gains)
    for bit in bits:
        gains = gains + pair(gains, bit)
    mask = 1
    while mask < n_t:
        gains = gains + across(gains, mask)
        mask *= 2
    return (
        block_out[None],
        in_grad[None],
        gains[0],
        w_qkv_grad,
        out_sum,
        gains[1],
        w_in_grad,
        mlp_sum[2],
    )


def solution(mesh):
    in_specs = (
        P("dp", "tensor", None),
        P("dp", "tensor"),
        P(),
        P(None, "dp", "tensor"),
        P("tensor", "dp"),
        P(),
        P(None, "dp", "tensor"),
        P("tensor", "dp"),
        P("dp", "tensor", None),
    )
    out_specs = (
        P("dp", "tensor", None),
        P("dp", "tensor", None),
        P(),
        P(None, "dp", "tensor"),
        P("tensor", "dp"),
        P(),
        P(None, "dp", "tensor"),
        P("tensor", "dp"),
    )
    return jax.shard_map(
        functools.partial(on_device, mesh.shape["dp"], mesh.shape["tensor"]),
        mesh=mesh,
        in_specs=in_specs,
        out_specs=out_specs,
        check_vma=False,
    )
```

```python
import functools

import jax
import jax.numpy as jnp
from jax import lax
from jax.experimental import pallas as pl
from jax.experimental.pallas import tpu as pltpu
from jax.sharding import PartitionSpec as P

HEAD_DIM = 64
HALF = HEAD_DIM // 2
EPSILON = 1e-05
ROPE_BASE = 160000.0
MASKED = -1e30
ROWS = 256
SCALE = HEAD_DIM ** (-0.5)
F32 = jnp.float32
BF16 = jnp.bfloat16


def dot(a, b, dims):
    return lax.dot_general(a, b, ((dims[0], dims[1]), ((), ())), preferred_element_type=F32)


NN = ((1,), (0,))
NT = ((1,), (1,))
TN = ((0,), (0,))


def spin(u, cosine, sine):
    width = u.shape[-1]
    lane = lax.broadcasted_iota(jnp.int32, u.shape, 1)
    other = jnp.where(
        lane % HEAD_DIM < HALF, pltpu.roll(u, width - HALF, 1), pltpu.roll(u, HALF, 1)
    )
    return u * cosine + other * sine


def head_mask(shape, head):
    lane = lax.broadcasted_iota(jnp.int32, shape, 1)
    return lane // HEAD_DIM == head


def attend_kernel(rows, normed, w_qkv, cosine, sine, seg_col, seg_row, q, k, v, ctx, lse):
    length, width = q.shape
    heads = width // HEAD_DIM

    @pl.loop(0, length // rows)
    def _(block):
        here = pl.ds(pl.multiple_of(block * rows, rows), rows)
        proj = dot(normed[here, :], w_qkv[...], NN)
        cos_here, sin_here = cosine[here, :], sine[here, :]
        q[here, :] = spin(proj[:, :width], cos_here, sin_here).astype(BF16)
        k[here, :] = spin(proj[:, width : 2 * width], cos_here, sin_here).astype(BF16)
        v[here, :] = proj[:, 2 * width :].astype(BF16)

    @pl.loop(0, length // rows)
    def _(block):
        here = pl.ds(pl.multiple_of(block * rows, rows), rows)
        q_here = q[here, :]
        same = seg_col[here, :] == seg_row[...]
        total = jnp.zeros((rows, width), F32)
        for head in range(heads):
            mine = head_mask((rows, width), head)
            q_head = jnp.where(mine, q_here, jnp.zeros_like(q_here)) * BF16(SCALE)
            scores = jnp.where(same, dot(q_head, k[...], NT), MASKED)
            highest = jnp.max(scores, axis=1, keepdims=True)
            weights = jnp.exp(scores - highest)
            sums = jnp.sum(weights, axis=1, keepdims=True)
            mixed = dot(weights.astype(BF16), v[...], NN) * (1.0 / sums)
            total = jnp.where(mine, mixed, total)
            lse[here, head : head + 1] = highest + jnp.log(sums)
        ctx[here, :] = total.astype(BF16)


def attend(normed, w_qkv, cosine, sine, seg_col, seg_row):
    length = normed.shape[0]
    width = w_qkv.shape[1] // 3
    rows = min(ROWS, length)
    heads = width // HEAD_DIM
    cost = pl.CostEstimate(
        flops=2 * length * normed.shape[1] * 3 * width + 4 * length * length * width * 4,
        bytes_accessed=8 * 2**20,
        transcendentals=heads * length * length,
    )
    wide = jax.ShapeDtypeStruct((length, width), BF16)
    return pl.pallas_call(
        functools.partial(attend_kernel, rows),
        out_shape=(wide, wide, wide, wide, jax.ShapeDtypeStruct((length, 128), F32)),
        compiler_params=pltpu.CompilerParams(vmem_limit_bytes=48 * 2**20),
        cost_estimate=cost,
        name="attend",
    )(normed, w_qkv, cosine, sine, seg_col, seg_row)


def attend_back_kernel(
    rows, dctx, q, k, v, lse_row, cosine, sine, seg_col, seg_row, dproj, dk_sum, dv_sum
):
    length, width = q.shape
    heads = width // HEAD_DIM
    dk_sum[...] = jnp.zeros_like(dk_sum)
    dv_sum[...] = jnp.zeros_like(dv_sum)

    @pl.loop(0, length // rows)
    def _(block):
        here = pl.ds(pl.multiple_of(block * rows, rows), rows)
        q_here, dctx_here = q[here, :], dctx[here, :]
        same = seg_col[...] == seg_row[:, here]
        dq = jnp.zeros((rows, width), F32)
        for head in range(heads):
            mine = head_mask((rows, width), head)
            q_head = jnp.where(mine, q_here, jnp.zeros_like(q_here)) * BF16(SCALE)
            dctx_head = jnp.where(mine, dctx_here, jnp.zeros_like(dctx_here))
            scores = jnp.where(same, dot(k[...], q_head, NT), MASKED)
            chances = jnp.exp(scores - lse_row[head : head + 1, here])
            grads = dot(v[...], dctx_head, NT)
            both = chances * grads
            inner = jnp.sum(both, axis=0, keepdims=True)
            dscores = (both - chances * inner).astype(BF16)
            dv_sum[...] += dot(chances.astype(BF16), dctx_head, NN)
            dk_sum[...] += dot(dscores, q_head, NN)
            dq = jnp.where(mine, dot(dscores, k[...], TN), dq)
        dq = spin(dq * SCALE, cosine[here, :], -sine[here, :])
        dproj[here, :width] = dq.astype(BF16)

    @pl.loop(0, length // rows)
    def _(block):
        here = pl.ds(pl.multiple_of(block * rows, rows), rows)
        dk = spin(dk_sum[here, :], cosine[here, :], -sine[here, :])
        dproj[here, width : 2 * width] = dk.astype(BF16)
        dproj[here, 2 * width :] = dv_sum[here, :].astype(BF16)


def attend_back(dctx, q, k, v, lse_row, cosine, sine, seg_col, seg_row):
    length, width = q.shape
    rows = min(ROWS, length)
    heads = width // HEAD_DIM
    cost = pl.CostEstimate(
        flops=10 * length * length * width * 4,
        bytes_accessed=8 * 2**20,
        transcendentals=heads * length * length,
    )
    return pl.pallas_call(
        functools.partial(attend_back_kernel, rows),
        out_shape=jax.ShapeDtypeStruct((length, 3 * width), BF16),
        scratch_shapes=[pltpu.VMEM((length, width), F32), pltpu.VMEM((length, width), F32)],
        compiler_params=pltpu.CompilerParams(vmem_limit_bytes=48 * 2**20),
        cost_estimate=cost,
        name="attend_back",
    )(dctx, q, k, v, lse_row, cosine, sine, seg_col, seg_row)


def normalize(rows):
    average = jnp.mean(rows, axis=-1, keepdims=True)
    centred = rows - average
    inv_std = lax.rsqrt(jnp.mean(centred * centred, axis=-1, keepdims=True) + EPSILON)
    return centred * inv_std, inv_std


def norm_back(grads, gain, scaled, inv_std):
    inner = grads * gain
    mean_grad = jnp.mean(inner, axis=-1, keepdims=True)
    mean_proj = jnp.mean(inner * scaled, axis=-1, keepdims=True)
    return inv_std * (inner - mean_grad - scaled * mean_proj)


def on_device(
    n_dp,
    n_t,
    block_in,
    segment_ids,
    norm1_gain,
    w_qkv,
    w_out,
    norm2_gain,
    w_in,
    w_mlp_out,
    out_grad,
):
    n_quad = n_dp // 2
    bits = [1 << b for b in range(n_quad.bit_length() - 1)]
    d_index, t_index = lax.axis_index("dp"), lax.axis_index("tensor")
    quad, first_core = d_index // 2, d_index % 2 == 0
    piece, d_model = block_in.shape[1], block_in.shape[2]
    length = piece * n_t
    width = w_qkv.shape[2]
    span = d_model // n_quad

    def core(x):
        return lax.ppermute(x, "dp", [(i, i ^ 1) for i in range(n_dp)])

    def pair(x, bit):
        return lax.ppermute(x, "dp", [(i, i ^ (2 * bit)) for i in range(n_dp)])

    def ahead(x, by):
        return lax.ppermute(x, "tensor", [(i, (i + by) % n_t) for i in range(n_t)])

    def across(x, mask):
        return lax.ppermute(x, "tensor", [(i, i ^ mask) for i in range(n_t)])

    def pick(a, b):
        return jnp.where(first_core, a, b)

    def reorder(x):
        cuts = [
            lax.dynamic_slice_in_dim(x, (quad ^ m) * span, span, axis=x.ndim - 1)
            for m in range(n_quad)
        ]
        return jnp.concatenate(cuts, axis=-1)

    def resume(side, values):
        with jax.named_scope(side["name"]):
            try:
                side["held"] = side["task"].send(values)
            except StopIteration as end:
                side.update(task=None, held=end.value)

    def begin(name, task):
        side = {"name": name, "task": task, "held": None}
        resume(side, None)
        return side

    def follow(chain, *sides):
        chain, held = lax.optimization_barrier((chain, [side["held"] for side in sides]))
        for side, values in zip(sides, held):
            side["held"] = values
            if side["task"] is not None:
                resume(side, values)
        return chain

    def finish(side):
        while side["task"] is not None:
            resume(side, side["held"])
        return side["held"]

    def pair_gather(x, orders):
        direct = yield {bit: pair(x, bit) for bit in bits}
        helds = [{0: x[i], order[0]: direct[order[0]][i]} for i, order in enumerate(orders)]
        for hop in range(1, len(bits)):
            turns = [order[hop] for order in orders]
            sent = yield [
                pair(jnp.stack([held[m] for m in sorted(held) if m]), bit)
                for held, bit in zip(helds, turns)
            ]
            for i, (held, bit) in enumerate(zip(helds, turns)):
                olds = sorted(m for m in held if m)
                held[bit] = direct[bit][i]
                held.update({m ^ bit: sent[i][n] for n, m in enumerate(olds)})
        return [[held[m] for m in range(n_quad)] for held in helds]

    def pair_scatter(lists, orders):
        helds = [dict(enumerate(blocks)) for blocks in lists]
        for hop in range(len(bits)):
            sent, kept = [], []
            for held, order in zip(helds, orders):
                stays = sorted(m for m in held if not m & order[hop])
                sent.append(pair(jnp.stack([held[m | order[hop]] for m in stays]), order[hop]))
                kept.append({m: held[m] for m in stays})
            sent, kept = yield sent, kept
            helds = [
                {
                    m: (stay[m].astype(F32) + come[n].astype(F32)).astype(BF16)
                    for n, m in enumerate(sorted(stay))
                }
                for stay, come in zip(kept, sent)
            ]
        return [held[0] for held in helds]

    def core_scatter(blocks):
        evens, odds = blocks[0::2], blocks[1::2]
        sent = core(jnp.stack([pick(b, a) for a, b in zip(evens, odds)]))
        kept = [pick(a, b) for a, b in zip(evens, odds)]
        sent, kept = yield sent, kept
        return [
            (stay.astype(F32) + sent[n].astype(F32)).astype(BF16) for n, stay in enumerate(kept)
        ]

    def ring_gather(x):
        return [x] + [ahead(x, -by) for by in range(1, n_t)]

    masks = list(range(0, n_t, 2))
    block = d_model // n_dp
    half = w_mlp_out.shape[0] // 2

    def qkv_weights(local):
        local = jnp.concatenate([local[0], local[1], local[2]], axis=1)
        (mine,) = yield from pair_gather(local[None], [bits])
        mine = jnp.stack(mine)
        mine, other = yield mine, core(mine)
        both = jnp.stack([pick(mine, other), pick(other, mine)], axis=1)
        return both.reshape(d_model, 3 * width)

    def out_weights(local, ids):
        ids = ids.astype(BF16).reshape(piece // block, block)
        tail = -ids.shape[0] % 16
        parts = yield ring_gather(jnp.concatenate([local, jnp.pad(ids, ((0, tail), (0, 0)))]))
        ids = [part[width : width + piece // block].reshape(1, piece) for part in parts]
        ids = jnp.concatenate(ids, axis=1).astype(jnp.int32)
        local = jnp.concatenate([part[:width] for part in parts], axis=0)
        ids, local = yield ids, local
        (mine,) = yield from pair_gather(local[None], [bits])
        mine = jnp.stack(mine)
        mine, other = yield mine, core(mine)
        first, second = pick(mine, other), pick(other, mine)
        return jnp.concatenate(
            [part for m in range(n_quad) for part in (first[m], second[m])], axis=1
        )

    def mlp_weights(local):
        even, odd = local[:, :half], local[:, half:]
        other = yield core(pick(odd, even))
        start = jnp.stack([pick(even, other), pick(other, odd)])
        lows, highs = yield from pair_gather(start, [bits[::-1], bits])
        return jnp.concatenate([part for both in zip(lows, highs) for part in both], axis=-1)

    def mlp_gradients(tokens, dy_tokens, acts):
        dact, dgate, prod = acts
        grads = jnp.stack(
            [
                dot(dact, tokens, TN).astype(BF16),
                dot(dgate, tokens, TN).astype(BF16),
                dot(prod, dy_tokens, TN).astype(BF16),
            ]
        )
        cuts = [grads[:, :, i * block : (i + 1) * block] for i in range(n_dp)]
        low, high = yield from pair_scatter([cuts[0::2], cuts[1::2]], [bits, bits[::-1]])
        own, other = yield pick(low, high), core(pick(high, low))
        first, second = pick(own, other), pick(other, own)
        ends = [
            jnp.concatenate([part[:, n * half : (n + 1) * half] for part in (first, second)], axis=1)
            for n in range(len(masks))
        ]
        moved = yield ends[:1] + [across(end, mask) for mask, end in zip(masks[1:], ends[1:])]
        return sum(end.astype(F32) for end in moved)

    def mlp_output(near, far):
        both = yield core(jnp.stack([near[piece:].astype(BF16), far[piece:].astype(BF16)]))
        back = yield across((far[:piece] + both[1].astype(F32)).astype(BF16), 1)
        return both[0].astype(F32) + back.astype(F32)

    def out_gradients(rows, grads):
        partial = dot(rows, grads, TN).astype(BF16)
        cuts = [partial[:, i * block : (i + 1) * block] for i in range(n_dp)]
        parts = yield from core_scatter(cuts)
        (low,) = yield from pair_scatter([parts], [bits])
        low = low.reshape(n_t, width, block)
        moved = yield [low[0]] + [ahead(low[s], s) for s in range(1, n_t)]
        return sum(part.astype(F32) for part in moved)

    def qkv_gradients(rows, grads):
        partial = dot(rows, grads, TN).astype(BF16)
        cuts = [partial[i * block : (i + 1) * block] for i in range(n_dp)]
        parts = yield from core_scatter(cuts)
        (total,) = yield from pair_scatter([parts], [bits])
        return total.astype(F32)

    def gain_gradients(parts):
        total = reorder(parts)
        hops = [core] + [functools.partial(pair, bit=bit) for bit in bits]
        hops += [functools.partial(across, mask=1 << i) for i in range(n_t.bit_length() - 1)]
        for hop in hops:
            total, other = yield total, hop(total)
            total = total + other
        return total

    x = reorder(block_in[0]).astype(F32)
    gain1, gain2 = reorder(norm1_gain), reorder(norm2_gain)
    scaled1, inv_std1 = normalize(x)
    own = (scaled1 * gain1).astype(BF16)
    own, later = lax.optimization_barrier(
        (own, (segment_ids, w_qkv, w_out, w_in, w_mlp_out, out_grad))
    )
    segment_ids, w_qkv, w_out, w_in, w_mlp_out, out_grad = later
    out_side = begin("out_weights", out_weights(w_out, segment_ids))
    qkv_side = begin("qkv_weights", qkv_weights(w_qkv))
    mlp_local = jnp.stack([w_in[0].T, w_in[1].T, w_mlp_out])
    mlp_sides = [begin("mlp_weights", mlp_weights(mlp_local))]
    low, high = [own], [own]
    for hop in range(1, n_t):
        ups = [(i, i + 1) for i in range(hop - 1, n_t - 1)]
        downs = [(n_t - 1 - i, n_t - 1 - j) for i, j in ups]
        with jax.named_scope("normed_gather"):
            low.append(lax.ppermute(low[-1], "tensor", ups))
            high.append(lax.ppermute(high[-1], "tensor", downs))
        if hop == 1:
            follow(0, out_side)
            segments = out_side["held"][0]
            places = (t_index * piece + jnp.arange(length, dtype=jnp.int32)) % length
            firsts = jnp.sum((segments < segments.reshape(length, 1)).astype(jnp.int32), axis=1)
            freqs = jnp.power(ROPE_BASE, -jnp.arange(HALF, dtype=F32) * 2.0 / HEAD_DIM)
            angles = (places - firsts).astype(F32)[:, None] * freqs[None, :]
            cosine, sine = jnp.cos(angles), jnp.sin(angles)
            cosine = jnp.tile(cosine, (1, width // HALF))
            sine = jnp.tile(jnp.concatenate([-sine, sine], axis=1), (1, width // HEAD_DIM))
            low[1], high[1], cosine, sine = follow(
                (low[1], high[1], cosine, sine), out_side, qkv_side, *mlp_sides
            )
        elif hop == 2:
            low[2], high[2], mlp_far = lax.optimization_barrier((low[2], high[2], mlp_local))
            with jax.named_scope("mlp_weights"):
                slices = [across(mlp_far, mask) for mask in masks[1:]]
            low[2], high[2] = follow((low[2], high[2]), out_side, qkv_side, *mlp_sides)
        elif hop == 3:
            low[3], high[3] = follow((low[3], high[3]), out_side, qkv_side)
            low[3], high[3], slices = lax.optimization_barrier((low[3], high[3], slices))
            mlp_sides += [begin("mlp_weights", mlp_weights(local)) for local in slices]
    normed = jnp.concatenate(
        [own] + [jnp.where(t_index + by < n_t, high[by], low[n_t - by]) for by in range(1, n_t)],
        axis=0,
    )
    normed = follow(normed, *mlp_sides[1:])
    qkv_full = finish(qkv_side)

    seg_col = segments.reshape(length, 1)
    q, k, v, ctx_local, lse = attend(normed, qkv_full, cosine, sine, seg_col, segments)
    lse_row = lse[:, : max(8, width // HEAD_DIM)].T

    dy = reorder(out_grad[0])
    with jax.named_scope("context"):
        ctx_pieces = [ahead(ctx_local[s * piece : (s + 1) * piece], s) for s in range(1, n_t)]
    with jax.named_scope("dy_tokens"):
        dy_moves = core(dy), across(dy, 1)
    ctx_local = follow(ctx_local, *mlp_sides)
    ctx_pieces = [ctx_local[:piece]] + ctx_pieces
    ctx = jnp.concatenate([ctx_pieces[(n_t - s) % n_t] for s in range(n_t)], axis=1)
    out_full = finish(out_side)
    hidden = x + dot(ctx, out_full, NN)

    scaled2, inv_std2 = normalize(hidden)
    normed2 = (scaled2 * gain2).astype(BF16)
    with jax.named_scope("normed2_tokens"):
        n2_core, n2_far = core(normed2), across(normed2, 1)
    with jax.named_scope("dy_tokens"):
        dy_near = jnp.concatenate([dy, dy_moves[0]])
        dy_far = jnp.concatenate([dy_moves[1], core(dy_moves[1])])
    with jax.named_scope("mlp_weights"):
        up, gate_up, down = (
            jnp.concatenate(parts) for parts in zip(*[finish(side) for side in mlp_sides])
        )

    def mlp_tokens(rows, dy_rows):
        act, gate = dot(rows, up, NT), dot(rows, gate_up, NT)
        dprod = dot(dy_rows, down, NT)
        below = 0.5 * (1.0 + lax.erf(act * (0.5**0.5)))
        slope = below + act * jnp.exp(-0.5 * act * act) * 0.3989422804014327
        gelu = act * below
        prod = (gelu * gate).astype(BF16)
        dact = (dprod * gate * slope).astype(BF16)
        dgate = (dprod * gelu).astype(BF16)
        return (dact, dgate, prod), dot(dact, up, NN) + dot(dgate, gate_up, NN)

    n2_near = jnp.concatenate([normed2, n2_core])
    near_acts, dn2_near = mlp_tokens(n2_near, dy_near)
    n2_far, near_acts, dn2_near = lax.optimization_barrier((n2_far, near_acts, dn2_near))
    with jax.named_scope("normed2_tokens"):
        n2_far = jnp.concatenate([n2_far, core(n2_far)])
    far_acts, dn2_far = mlp_tokens(n2_far, dy_far)
    with jax.named_scope("dn2_tokens"):
        dn2_core = core(jnp.stack([dn2_near[piece:].astype(BF16), dn2_far[piece:].astype(BF16)]))
        dn2_core, near_acts, far_acts = lax.optimization_barrier((dn2_core, near_acts, far_acts))
        dn2_back = across((dn2_far[:piece] + dn2_core[1].astype(F32)).astype(BF16), 1)
    grads_side = begin(
        "mlp_grads",
        mlp_gradients(
            jnp.concatenate([n2_near, n2_far]),
            jnp.concatenate([dy_near, dy_far]),
            [jnp.concatenate(both) for both in zip(near_acts, far_acts)],
        ),
    )
    dn2_own = dn2_near[:piece] + dn2_core[0].astype(F32) + dn2_back.astype(F32)
    dh = dy.astype(F32) + norm_back(dn2_own, gain2, scaled2, inv_std2)
    gain2_part = jnp.sum(dn2_own * scaled2, axis=0)
    dh_low = dh.astype(BF16)

    dctx = dot(dh_low, out_full, NT).astype(BF16)
    with jax.named_scope("dctx"):
        dctx_pieces = [ahead(dctx[:, s * width : (s + 1) * width], s) for s in range(1, n_t)]

    dctx, near_prod, far_prod, ctx, dh_side = lax.optimization_barrier(
        (dctx, near_acts[2], far_acts[2], ctx, dh_low)
    )
    with jax.named_scope("mlp_out"):
        mlp_near, mlp_far = dot(near_prod, down, NN), dot(far_prod, down, NN)
    mlp_side = begin("mlp_out", mlp_output(mlp_near, mlp_far))
    out_side = begin("out_grads", out_gradients(ctx, dh_side))
    dctx_pieces = [dctx[:, :width]] + dctx_pieces
    dctx_local = jnp.concatenate([dctx_pieces[(n_t - s) % n_t] for s in range(n_t)], axis=0)
    dctx_local = follow(dctx_local, out_side, mlp_side)
    dproj = attend_back(dctx_local, q, k, v, lse_row, cosine, sine, seg_col, segments)
    dn1 = dot(dproj, qkv_full, NT)
    gain1_part = jnp.sum(dn1 * normed.astype(F32), axis=0) / gain1
    dn1_low = dn1.astype(BF16)
    cuts = [dn1_low[s * piece : (s + 1) * piece] for s in range(n_t)]
    with jax.named_scope("dn1_sum"):
        highs = lax.ppermute(cuts[n_t - 1], "tensor", [(0, 1)])
        lows = lax.ppermute(cuts[1], "tensor", [(n_t - 1, n_t - 2)])
    dproj = follow(dproj, grads_side, out_side)
    cuts, dproj, normed = lax.optimization_barrier((cuts, dproj, normed))
    qkv_side = begin("qkv_grads", qkv_gradients(normed, dproj))
    gains_side = begin("gains", gain_gradients(jnp.stack([gain1_part, gain2_part])))
    for hop in range(2, n_t):
        lows, highs = follow((lows, highs), gains_side, qkv_side)
        with jax.named_scope("dn1_sum"):
            ups = [(i, i + 1) for i in range(hop)]
            downs = [(n_t - 1 - i, n_t - 1 - j) for i, j in ups]
            lows = (cuts[hop].astype(F32) + lows.astype(F32)).astype(BF16)
            highs = (cuts[n_t - hop].astype(F32) + highs.astype(F32)).astype(BF16)
            lows, highs = lax.ppermute(lows, "tensor", downs), lax.ppermute(highs, "tensor", ups)
        cuts = follow(cuts, gains_side, grads_side, out_side)
    lows, highs = follow((lows, highs), gains_side, qkv_side, mlp_side)
    dn1_own = cuts[0].astype(F32) + lows.astype(F32) + highs.astype(F32)
    in_grad = reorder(dh + norm_back(dn1_own, gain1, scaled1, inv_std1))
    block_out = reorder((hidden + mlp_near[:piece] + finish(mlp_side)).astype(BF16))

    gains = finish(gains_side)
    mlp_sum = finish(grads_side)
    qkv_sum = finish(qkv_side)
    w_qkv_grad = jnp.stack([qkv_sum[:, c * width : (c + 1) * width] for c in range(3)])
    return (
        block_out[None],
        in_grad[None],
        gains[0],
        w_qkv_grad,
        finish(out_side),
        gains[1],
        jnp.stack([mlp_sum[0].T, mlp_sum[1].T]),
        mlp_sum[2],
    )


def solution(mesh):
    in_specs = (
        P("dp", "tensor", None),
        P("dp", "tensor"),
        P(),
        P(None, "dp", "tensor"),
        P("tensor", "dp"),
        P(),
        P(None, "dp", "tensor"),
        P("tensor", "dp"),
        P("dp", "tensor", None),
    )
    out_specs = (
        P("dp", "tensor", None),
        P("dp", "tensor", None),
        P(),
        P(None, "dp", "tensor"),
        P("tensor", "dp"),
        P(),
        P(None, "dp", "tensor"),
        P("tensor", "dp"),
    )
    return jax.shard_map(
        functools.partial(on_device, mesh.shape["dp"], mesh.shape["tensor"]),
        mesh=mesh,
        in_specs=in_specs,
        out_specs=out_specs,
        check_vma=False,
    )
```

```python
import functools

import jax
import jax.numpy as jnp
from jax import lax
from jax.experimental import pallas as pl
from jax.experimental.pallas import tpu as pltpu
from jax.sharding import PartitionSpec as P

HEAD_DIM = 64
HALF = HEAD_DIM // 2
EPSILON = 1e-05
ROPE_BASE = 160000.0
MASKED = -1e30
ROWS = 256
SCALE = HEAD_DIM ** (-0.5)
F32 = jnp.float32
BF16 = jnp.bfloat16


def dot(a, b, dims):
    return lax.dot_general(a, b, ((dims[0], dims[1]), ((), ())), preferred_element_type=F32)


NN = ((1,), (0,))
NT = ((1,), (1,))
TN = ((0,), (0,))


def spin(u, cosine, sine):
    width = u.shape[-1]
    times = width // cosine.shape[-1]
    cosine, sine = (jnp.concatenate([table] * times, axis=1) for table in (cosine, sine))
    lane = lax.broadcasted_iota(jnp.int32, u.shape, 1)
    other = jnp.where(
        lane % HEAD_DIM < HALF, pltpu.roll(u, width - HALF, 1), pltpu.roll(u, HALF, 1)
    )
    return u * cosine + other * sine


def head_mask(shape, head):
    lane = lax.broadcasted_iota(jnp.int32, shape, 1)
    return lane // HEAD_DIM == head


def attend_kernel(rows, n_t, place, own, *refs):
    lows, highs = refs[: n_t - 1], refs[n_t - 1 : 2 * n_t - 2]
    mine, other, cosine, sine, seg_col, seg_row = refs[2 * n_t - 2 : 2 * n_t + 4]
    q, k, v, ctx, lse, normed, w_qkv = refs[2 * n_t + 4 :]
    length, width = q.shape
    piece = own.shape[0]
    heads = width // HEAD_DIM
    block_rows = mine.shape[1]

    normed[:piece, :] = own[...]
    for by in range(1, n_t):
        there = slice(by * piece, (by + 1) * piece)

        @pl.when(place[0] + by < n_t)
        def _(there=there, by=by):
            normed[there, :] = highs[by - 1][...]

        @pl.when(place[0] + by >= n_t)
        def _(there=there, by=by):
            normed[there, :] = lows[n_t - by - 1][...]

    for m in range(mine.shape[0]):
        even = slice(2 * m * block_rows, (2 * m + 1) * block_rows)
        odd = slice((2 * m + 1) * block_rows, (2 * m + 2) * block_rows)

        @pl.when(place[1] == 0)
        def _(m=m, even=even, odd=odd):
            w_qkv[even, :] = mine[m]
            w_qkv[odd, :] = other[m]

        @pl.when(place[1] == 1)
        def _(m=m, even=even, odd=odd):
            w_qkv[even, :] = other[m]
            w_qkv[odd, :] = mine[m]

    @pl.loop(0, length // rows)
    def _(block):
        here = pl.ds(pl.multiple_of(block * rows, rows), rows)
        proj = dot(normed[here, :], w_qkv[...], NN)
        cos_here, sin_here = cosine[here, :], sine[here, :]
        q[here, :] = spin(proj[:, :width], cos_here, sin_here).astype(BF16)
        k[here, :] = spin(proj[:, width : 2 * width], cos_here, sin_here).astype(BF16)
        v[here, :] = proj[:, 2 * width :].astype(BF16)

    @pl.loop(0, length // rows)
    def _(block):
        here = pl.ds(pl.multiple_of(block * rows, rows), rows)
        q_here = q[here, :]
        same = seg_col[here, :] == seg_row[...]
        total = jnp.zeros((rows, width), F32)
        for head in range(heads):
            mine = head_mask((rows, width), head)
            q_head = jnp.where(mine, q_here, jnp.zeros_like(q_here)) * BF16(SCALE)
            scores = jnp.where(same, dot(q_head, k[...], NT), MASKED)
            highest = jnp.max(scores, axis=1, keepdims=True)
            weights = jnp.exp(scores - highest)
            sums = jnp.sum(weights, axis=1, keepdims=True)
            mixed = dot(weights.astype(BF16), v[...], NN) * (1.0 / sums)
            total = jnp.where(mine, mixed, total)
            lse[here, head : head + 1] = highest + jnp.log(sums)
        ctx[here, :] = total.astype(BF16)


def attend(place, lows, highs, mine, other, cosine, sine, seg_col, seg_row):
    length, width = cosine.shape[0], mine.shape[-1] // 3
    d_model = lows[0].shape[1]
    rows = min(ROWS, length)
    heads = width // HEAD_DIM
    cost = pl.CostEstimate(
        flops=2 * length * d_model * 3 * width + 4 * length * length * width * 4,
        bytes_accessed=8 * 2**20,
        transcendentals=heads * length * length,
    )
    wide = jax.ShapeDtypeStruct((length, width), BF16)
    whole = pl.BlockSpec()
    arrays = (*lows, *highs[1:], mine, other, cosine, sine, seg_col, seg_row)
    return pl.pallas_call(
        functools.partial(attend_kernel, rows, len(lows)),
        in_specs=[pl.BlockSpec(memory_space=pltpu.SMEM)] + [whole] * len(arrays),
        out_specs=[whole] * 7,
        out_shape=(
            wide,
            wide,
            wide,
            wide,
            jax.ShapeDtypeStruct((length, 128), F32),
            jax.ShapeDtypeStruct((length, d_model), BF16),
            jax.ShapeDtypeStruct((d_model, 3 * width), BF16),
        ),
        compiler_params=pltpu.CompilerParams(vmem_limit_bytes=48 * 2**20),
        cost_estimate=cost,
        name="attend",
    )(place, *arrays)


def attend_back_kernel(
    rows, dctx, q, k, v, lse_row, cosine, sine, seg_col, seg_row, dproj, dk_sum, dv_sum
):
    length, width = q.shape
    heads = width // HEAD_DIM
    dk_sum[...] = jnp.zeros_like(dk_sum)
    dv_sum[...] = jnp.zeros_like(dv_sum)

    @pl.loop(0, length // rows)
    def _(block):
        here = pl.ds(pl.multiple_of(block * rows, rows), rows)
        q_here, dctx_here = q[here, :], dctx[here, :]
        same = seg_col[...] == seg_row[:, here]
        dq = jnp.zeros((rows, width), F32)
        for head in range(heads):
            mine = head_mask((rows, width), head)
            q_head = jnp.where(mine, q_here, jnp.zeros_like(q_here)) * BF16(SCALE)
            dctx_head = jnp.where(mine, dctx_here, jnp.zeros_like(dctx_here))
            scores = jnp.where(same, dot(k[...], q_head, NT), MASKED)
            chances = jnp.exp(scores - lse_row[head : head + 1, here])
            grads = dot(v[...], dctx_head, NT)
            both = chances * grads
            inner = jnp.sum(both, axis=0, keepdims=True)
            dscores = (both - chances * inner).astype(BF16)
            dv_sum[...] += dot(chances.astype(BF16), dctx_head, NN)
            dk_sum[...] += dot(dscores, q_head, NN)
            dq = jnp.where(mine, dot(dscores, k[...], TN), dq)
        dq = spin(dq * SCALE, cosine[here, :], -sine[here, :])
        dproj[here, :width] = dq.astype(BF16)

    @pl.loop(0, length // rows)
    def _(block):
        here = pl.ds(pl.multiple_of(block * rows, rows), rows)
        dk = spin(dk_sum[here, :], cosine[here, :], -sine[here, :])
        dproj[here, width : 2 * width] = dk.astype(BF16)
        dproj[here, 2 * width :] = dv_sum[here, :].astype(BF16)


def attend_back(dctx, q, k, v, lse_row, cosine, sine, seg_col, seg_row):
    length, width = q.shape
    rows = min(ROWS, length)
    heads = width // HEAD_DIM
    cost = pl.CostEstimate(
        flops=10 * length * length * width * 4,
        bytes_accessed=8 * 2**20,
        transcendentals=heads * length * length,
    )
    return pl.pallas_call(
        functools.partial(attend_back_kernel, rows),
        out_shape=jax.ShapeDtypeStruct((length, 3 * width), BF16),
        scratch_shapes=[pltpu.VMEM((length, width), F32), pltpu.VMEM((length, width), F32)],
        compiler_params=pltpu.CompilerParams(vmem_limit_bytes=48 * 2**20),
        cost_estimate=cost,
        name="attend_back",
    )(dctx, q, k, v, lse_row, cosine, sine, seg_col, seg_row)


def normalize(rows):
    average = jnp.mean(rows, axis=-1, keepdims=True)
    centred = rows - average
    inv_std = lax.rsqrt(jnp.mean(centred * centred, axis=-1, keepdims=True) + EPSILON)
    return centred * inv_std, inv_std


def norm_back(grads, gain, scaled, inv_std):
    inner = grads * gain
    mean_grad = jnp.mean(inner, axis=-1, keepdims=True)
    mean_proj = jnp.mean(inner * scaled, axis=-1, keepdims=True)
    return inv_std * (inner - mean_grad - scaled * mean_proj)


def on_device(
    n_dp,
    n_t,
    block_in,
    segment_ids,
    norm1_gain,
    w_qkv,
    w_out,
    norm2_gain,
    w_in,
    w_mlp_out,
    out_grad,
):
    n_quad = n_dp // 2
    bits = [1 << b for b in range(n_quad.bit_length() - 1)]
    d_index, t_index = lax.axis_index("dp"), lax.axis_index("tensor")
    quad, first_core = d_index // 2, d_index % 2 == 0
    piece, d_model = block_in.shape[1], block_in.shape[2]
    length = piece * n_t
    width = w_qkv.shape[2]
    span = d_model // n_quad

    def core(x):
        return lax.ppermute(x, "dp", [(i, i ^ 1) for i in range(n_dp)])

    def pair(x, bit):
        return lax.ppermute(x, "dp", [(i, i ^ (2 * bit)) for i in range(n_dp)])

    def ahead(x, by):
        return lax.ppermute(x, "tensor", [(i, (i + by) % n_t) for i in range(n_t)])

    def across(x, mask):
        return lax.ppermute(x, "tensor", [(i, i ^ mask) for i in range(n_t)])

    def pick(a, b):
        return jnp.where(first_core, a, b)

    def reorder(x):
        cuts = [
            lax.dynamic_slice_in_dim(x, (quad ^ m) * span, span, axis=x.ndim - 1)
            for m in range(n_quad)
        ]
        return jnp.concatenate(cuts, axis=-1)

    def resume(side, values):
        with jax.named_scope(side["name"]):
            try:
                side["held"] = side["task"].send(values)
            except StopIteration as end:
                side.update(task=None, held=end.value)

    def begin(name, task):
        side = {"name": name, "task": task, "held": None}
        resume(side, None)
        return side

    def hold(chain, *sides):
        chain, held = lax.optimization_barrier((chain, [side["held"] for side in sides]))
        for side, values in zip(sides, held):
            side["held"] = values
        return chain

    def follow(chain, *sides):
        chain = hold(chain, *sides)
        for side in sides:
            if side["task"] is not None:
                resume(side, side["held"])
        return chain

    def wait_for(marker, values):
        return lax.optimization_barrier((marker, values))[1]

    def finish(side):
        while side["task"] is not None:
            resume(side, side["held"])
        return side["held"]

    def pair_turn(x, hop, flip=0):
        steps = [(bits[hop], bits[::-1][hop])[(i + flip) % 2] for i in range(n_dp)]
        return lax.ppermute(x, "dp", [(i, i ^ (2 * steps[i])) for i in range(n_dp)])

    def pair_gather(x, flip=0):
        held, labels = [x], [[0], [0]]
        orders = (bits[::-1], bits) if flip else (bits, bits[::-1])
        for hop in range(len(bits)):
            sent = yield pair_turn(jnp.stack(held), hop, flip)
            held = held + [sent[n] for n in range(len(held))]
            labels = [
                some + [m ^ order[hop] for m in some]
                for some, order in zip(labels, orders)
            ]
        places = [[some.index(m) for m in range(n_quad)] for some in labels]
        return [held[a] if a == b else pick(held[a], held[b]) for a, b in zip(*places)]

    def pair_scatter(blocks):
        held, labels = list(blocks), [list(range(n_quad))] * 2

        def chosen(wanted):
            spots = [[some.index(m) for m in want] for some, want in zip(labels, wanted)]
            return [held[a] if a == b else pick(held[a], held[b]) for a, b in zip(*spots)]

        for hop in range(len(bits)):
            turns = bits[hop], bits[::-1][hop]
            stays = [[m for m in some if not m & bit] for some, bit in zip(labels, turns)]
            goes = [[m | bit for m in some] for some, bit in zip(stays, turns)]
            sent, kept = yield pair_turn(jnp.stack(chosen(goes)), hop), chosen(stays)
            held = [
                (stay.astype(F32) + sent[n].astype(F32)).astype(BF16)
                for n, stay in enumerate(kept)
            ]
            labels = stays
        return held[0]

    def core_scatter(blocks):
        evens, odds = blocks[0::2], blocks[1::2]
        sent = core(jnp.stack([pick(b, a) for a, b in zip(evens, odds)]))
        kept = [pick(a, b) for a, b in zip(evens, odds)]
        sent, kept = yield sent, kept
        return [
            (stay.astype(F32) + sent[n].astype(F32)).astype(BF16) for n, stay in enumerate(kept)
        ]

    doublings = [1 << i for i in range(n_t.bit_length() - 1)]

    def line_swaps(x):
        held = [x]
        for mask in doublings:
            sent = yield across(jnp.stack(held), mask)
            held = held + [sent[n] for n in range(len(held))]
        return held

    def line_scatter(held):
        for mask in doublings[::-1]:
            sent, held = yield across(jnp.stack(held[mask:]), mask), held[:mask]
            held = [
                (stay.astype(F32) + sent[n].astype(F32)).astype(BF16)
                for n, stay in enumerate(held)
            ]
        return held[0]

    def to_line(held):
        held = jnp.stack(held)
        return [
            lax.dynamic_index_in_dim(held, t_index ^ ((t_index + s) % n_t), 0, False)
            for s in range(n_t)
        ]

    def from_line(held):
        return [
            lax.dynamic_index_in_dim(held, ((t_index ^ m) - t_index) % n_t, 0, False)
            for m in range(n_t)
        ]

    masks = list(range(0, n_t, 2))
    block = d_model // n_dp
    half = w_mlp_out.shape[0] // 2

    def qkv_weights(local):
        local = jnp.concatenate([local[0], local[1], local[2]], axis=1)
        mine = yield from pair_gather(local)
        mine = jnp.stack(mine)
        mine, other = yield mine, core(mine)
        return mine, other

    def out_rows(local, ids):
        ids = ids.astype(BF16).reshape(piece // block, block)
        tail = -ids.shape[0] % 16
        packed = jnp.concatenate([local, jnp.pad(ids, ((0, tail), (0, 0)))])
        return [packed] + [ahead(packed, -by) for by in range(1, n_t)]

    def out_weights(local):
        mine = yield from pair_gather(local, 1)
        mine = jnp.stack(mine)
        mine, other = yield mine, core(mine)
        first, second = pick(mine, other), pick(other, mine)
        return jnp.concatenate(
            [part for m in range(n_quad) for part in (first[m], second[m])], axis=1
        )

    def mlp_weights(local):
        even, odd = local[:, :half], local[:, half:]
        other = yield core(pick(odd, even))
        start = jnp.concatenate([pick(even, other), pick(other, odd)], axis=-1)
        blocks = yield from pair_gather(start)
        return jnp.concatenate(blocks, axis=-1)

    def mlp_gradients(tokens, dy_tokens, acts):
        dact, dgate, prod = acts
        grads = jnp.stack(
            [
                dot(dact, tokens, TN).astype(BF16),
                dot(dgate, tokens, TN).astype(BF16),
                dot(prod, dy_tokens, TN).astype(BF16),
            ]
        )
        total = yield from pair_scatter(
            [grads[:, :, m * span : (m + 1) * span] for m in range(n_quad)]
        )
        low, high = total[..., :block], total[..., block:]
        own, other = yield pick(low, high), core(pick(high, low))
        first, second = pick(own, other), pick(other, own)
        ends = [
            jnp.concatenate([part[:, n * half : (n + 1) * half] for part in (first, second)], axis=1)
            for n in range(len(masks))
        ]
        moved = yield ends[:1] + [across(end, mask) for mask, end in zip(masks[1:], ends[1:])]
        return sum(end.astype(F32) for end in moved)

    def mlp_output(near, far):
        both = yield core(jnp.stack([near[piece:].astype(BF16), far[piece:].astype(BF16)]))
        back = yield across((far[:piece] + both[1].astype(F32)).astype(BF16), 1)
        return both[0].astype(F32) + back.astype(F32)

    def out_gradients(rows, grads):
        partial = dot(rows, grads, TN).astype(BF16)
        cuts = [partial[:, i * block : (i + 1) * block] for i in range(n_dp)]
        parts = yield from core_scatter(cuts)
        low = yield from pair_scatter(parts)
        total = yield from line_scatter(from_line(low.reshape(n_t, width, block)))
        return total.astype(F32)

    def qkv_gradients(rows, grads):
        partial = dot(rows, grads, TN).astype(BF16)
        cuts = [partial[i * block : (i + 1) * block] for i in range(n_dp)]
        parts = yield from core_scatter(cuts)
        total = yield from pair_scatter(parts)
        return total.astype(F32)

    def gain_gradients(parts):
        total = reorder(parts)
        hops = [functools.partial(across, mask=mask) for mask in doublings] + [core]
        hops += [functools.partial(pair, bit=bit) for bit in bits]
        for hop in hops:
            total, other = yield total, hop(total)
            total = total + other
        return total

    x = reorder(block_in[0]).astype(F32)
    gain1, gain2 = reorder(norm1_gain), reorder(norm2_gain)
    scaled1, inv_std1 = normalize(x)
    own = (scaled1 * gain1).astype(BF16)
    with jax.named_scope("out_weights"):
        rows = out_rows(w_out, segment_ids)
    own, w_qkv, w_in, w_mlp_out, out_grad = wait_for(
        rows[1:], (own, w_qkv, w_in, w_mlp_out, out_grad)
    )
    ids = [part[width : width + piece // block].reshape(1, piece) for part in rows]
    segments = jnp.concatenate(ids, axis=1).astype(jnp.int32)
    out_local = jnp.concatenate([part[:width] for part in rows], axis=0)
    qkv_side = begin("qkv_weights", qkv_weights(w_qkv))
    mlp_local = jnp.stack([w_in[0].T, w_in[1].T, w_mlp_out])
    mlp_sides = [begin("mlp_weights", mlp_weights(mlp_local))]
    resume(mlp_sides[0], mlp_sides[0]["held"])
    low, high = [own], [own]
    for hop in range(1, n_t):
        ups = [(i, i + 1) for i in range(hop - 1, n_t - 1)]
        downs = [(n_t - 1 - i, n_t - 1 - j) for i, j in ups]
        with jax.named_scope("normed_gather"):
            low.append(lax.ppermute(low[-1], "tensor", ups))
            high.append(lax.ppermute(high[-1], "tensor", downs))
        if hop == 1:
            low[1], high[1], mlp_far = follow((low[1], high[1], mlp_local), qkv_side)
            with jax.named_scope("mlp_weights"):
                slices = [across(mlp_far, mask) for mask in masks[1:]]
            places = (t_index * piece + jnp.arange(length, dtype=jnp.int32)) % length
            firsts = jnp.sum((segments < segments.reshape(length, 1)).astype(jnp.int32), axis=1)
            freqs = jnp.power(ROPE_BASE, -jnp.arange(HALF, dtype=F32) * 2.0 / HEAD_DIM)
            angles = (places - firsts).astype(F32)[:, None] * freqs[None, :]
            cosine, sine = jnp.cos(angles), jnp.sin(angles)
            cosine = jnp.tile(cosine, (1, 4))
            sine = jnp.tile(jnp.concatenate([-sine, sine], axis=1), (1, 2))
        elif hop == 2:
            low[2], high[2], cosine, sine, out_local, out_grad = follow(
                hold((low[2], high[2], cosine, sine, out_local, out_grad), mlp_sides[0]), qkv_side
            )
            out_side = begin("out_weights", out_weights(out_local))
        elif hop == 3:
            low[3], high[3], slices = follow(
                (low[3], high[3], slices), out_side, qkv_side, mlp_sides[0]
            )
            mlp_sides += [begin("mlp_weights", mlp_weights(local)) for local in slices]
    dy = reorder(out_grad[0])
    with jax.named_scope("dy_tokens"):
        dy_moves = core(dy), across(dy, 1)
    high[-1] = follow(high[-1], *mlp_sides[1:])

    place = jnp.stack([t_index, d_index % 2]).astype(jnp.int32)
    seg_col = segments.reshape(length, 1)
    q, k, v, ctx_local, lse, normed, qkv_full = attend(
        place, low, high, *finish(qkv_side), cosine, sine, seg_col, segments
    )
    lse_row = lse[:, : max(8, width // HEAD_DIM)].T

    ctx_local, dy_moves = follow((ctx_local, dy_moves), out_side, *mlp_sides)
    with jax.named_scope("context"):
        ctx_pieces = [ahead(ctx_local[s * piece : (s + 1) * piece], s) for s in range(1, n_t)]
    ctx_pieces = [ctx_local[:piece]] + ctx_pieces
    ctx = jnp.concatenate([ctx_pieces[(n_t - s) % n_t] for s in range(n_t)], axis=1)
    out_full = finish(out_side)
    hidden = x + dot(ctx, out_full, NN)

    scaled2, inv_std2 = normalize(hidden)
    normed2 = (scaled2 * gain2).astype(BF16)
    with jax.named_scope("normed2_tokens"):
        n2_core, n2_far = core(normed2), across(normed2, 1)
    with jax.named_scope("dy_tokens"):
        dy_near = jnp.concatenate([dy, dy_moves[0]])
        dy_far = wait_for(n2_core, dy_moves[1])
        dy_far = jnp.concatenate([dy_far, core(dy_far)])
    with jax.named_scope("mlp_weights"):
        for side in mlp_sides[1:]:
            side["held"] = wait_for(n2_core, side["held"])
        up, gate_up, down = (
            jnp.concatenate(parts) for parts in zip(*[finish(side) for side in mlp_sides])
        )

    def mlp_tokens(rows, dy_rows):
        act, gate = dot(rows, up, NT), dot(rows, gate_up, NT)
        dprod = dot(dy_rows, down, NT)
        below = 0.5 * (1.0 + lax.erf(act * (0.5**0.5)))
        slope = below + act * jnp.exp(-0.5 * act * act) * 0.3989422804014327
        gelu = act * below
        prod = (gelu * gate).astype(BF16)
        dact = (dprod * gate * slope).astype(BF16)
        dgate = (dprod * gelu).astype(BF16)
        return (dact, dgate, prod), dot(dact, up, NN) + dot(dgate, gate_up, NN)

    n2_near = jnp.concatenate([normed2, n2_core])
    near_acts, dn2_near = mlp_tokens(n2_near, dy_near)
    n2_far, near_acts, dn2_near = lax.optimization_barrier((n2_far, near_acts, dn2_near))
    with jax.named_scope("normed2_tokens"):
        n2_far = jnp.concatenate([n2_far, core(n2_far)])
    far_acts, dn2_far = mlp_tokens(n2_far, dy_far)
    with jax.named_scope("dn2_tokens"):
        dn2_core = core(jnp.stack([dn2_near[piece:].astype(BF16), dn2_far[piece:].astype(BF16)]))
        dn2_send = (dn2_far[:piece] + dn2_core[1].astype(F32)).astype(BF16)
        dn2_send, near_acts, far_acts = lax.optimization_barrier((dn2_send, near_acts, far_acts))
        dn2_back = across(dn2_send, 1)
    grads_side = begin(
        "mlp_grads",
        mlp_gradients(
            jnp.concatenate([n2_near, n2_far]),
            jnp.concatenate([dy_near, dy_far]),
            [jnp.concatenate(both) for both in zip(near_acts, far_acts)],
        ),
    )
    with jax.named_scope("mlp_out"):
        mlp_near, mlp_far = dot(near_acts[2], down, NN), dot(far_acts[2], down, NN)
    mlp_side = begin("mlp_out", mlp_output(mlp_near, mlp_far))
    dn2_own = dn2_near[:piece] + dn2_core[0].astype(F32) + dn2_back.astype(F32)
    dh = dy.astype(F32) + norm_back(dn2_own, gain2, scaled2, inv_std2)
    gain2_part = jnp.sum(dn2_own * scaled2, axis=0)
    dh_low = dh.astype(BF16)

    dctx = dot(dh_low, out_full, NT).astype(BF16)
    with jax.named_scope("dctx"):
        dctx_pieces = [ahead(dctx[:, s * width : (s + 1) * width], s) for s in range(1, n_t)]

    out_side = begin("out_grads", out_gradients(ctx, dh_low))
    dctx_pieces = [dctx[:, :width]] + dctx_pieces
    dctx_local = jnp.concatenate([dctx_pieces[(n_t - s) % n_t] for s in range(n_t)], axis=0)
    dctx_local = follow(dctx_local, out_side, mlp_side)
    dproj = attend_back(dctx_local, q, k, v, lse_row, cosine, sine, seg_col, segments)
    dn1 = dot(dproj, qkv_full, NT)
    gain1_part = jnp.sum(dn1 * normed.astype(F32), axis=0) / gain1
    dn1_low = dn1.astype(BF16)
    cuts = [dn1_low[s * piece : (s + 1) * piece] for s in range(n_t)]
    with jax.named_scope("dn1_sum"):
        highs = lax.ppermute(cuts[n_t - 1], "tensor", [(0, 1)])
        lows = lax.ppermute(cuts[1], "tensor", [(n_t - 1, n_t - 2)])
    dproj = follow(hold(dproj, out_side), grads_side, mlp_side)
    cuts, dproj, normed = lax.optimization_barrier((cuts, dproj, normed))
    gains_side = begin("gains", gain_gradients(jnp.stack([gain1_part, gain2_part])))
    qkv_side = begin("qkv_grads", qkv_gradients(normed, dproj))
    for hop in range(2, n_t):
        if hop == 2:
            lows, highs = follow((lows, highs), gains_side, qkv_side, out_side)
        else:
            lows, highs = follow((lows, highs), grads_side, gains_side, out_side)
            out_side["held"] = follow(out_side["held"], qkv_side)
        with jax.named_scope("dn1_sum"):
            ups = [(i, i + 1) for i in range(hop)]
            downs = [(n_t - 1 - i, n_t - 1 - j) for i, j in ups]
            lows = (cuts[hop].astype(F32) + lows.astype(F32)).astype(BF16)
            highs = (cuts[n_t - hop].astype(F32) + highs.astype(F32)).astype(BF16)
            lows, highs = lax.ppermute(lows, "tensor", downs), lax.ppermute(highs, "tensor", ups)
        if hop == 2:
            cuts = follow(cuts, grads_side)
    lows, highs = follow((lows, highs), grads_side)
    dn1_own = cuts[0].astype(F32) + lows.astype(F32) + highs.astype(F32)
    in_grad = reorder(dh + norm_back(dn1_own, gain1, scaled1, inv_std1))
    block_out = reorder((hidden + mlp_near[:piece] + finish(mlp_side)).astype(BF16))

    gains = finish(gains_side)
    mlp_sum = finish(grads_side)
    qkv_sum = finish(qkv_side)
    w_qkv_grad = jnp.stack([qkv_sum[:, c * width : (c + 1) * width] for c in range(3)])
    return (
        block_out[None],
        in_grad[None],
        gains[0],
        w_qkv_grad,
        finish(out_side),
        gains[1],
        jnp.stack([mlp_sum[0].T, mlp_sum[1].T]),
        mlp_sum[2],
    )


def solution(mesh):
    in_specs = (
        P("dp", "tensor", None),
        P("dp", "tensor"),
        P(),
        P(None, "dp", "tensor"),
        P("tensor", "dp"),
        P(),
        P(None, "dp", "tensor"),
        P("tensor", "dp"),
        P("dp", "tensor", None),
    )
    out_specs = (
        P("dp", "tensor", None),
        P("dp", "tensor", None),
        P(),
        P(None, "dp", "tensor"),
        P("tensor", "dp"),
        P(),
        P(None, "dp", "tensor"),
        P("tensor", "dp"),
    )
    return jax.shard_map(
        functools.partial(on_device, mesh.shape["dp"], mesh.shape["tensor"]),
        mesh=mesh,
        in_specs=in_specs,
        out_specs=out_specs,
        check_vma=False,
    )
```

```python
import functools

import jax
import jax.numpy as jnp
from jax import lax
from jax.experimental import pallas as pl
from jax.experimental.pallas import tpu as pltpu
from jax.sharding import PartitionSpec as P

HEAD_DIM = 64
HALF = HEAD_DIM // 2
EPSILON = 1e-05
ROPE_BASE = 160000.0
MASKED = -1e30
ROWS = 512
SCALE = HEAD_DIM ** (-0.5)
F32 = jnp.float32
BF16 = jnp.bfloat16


def dot(a, b, dims):
    return lax.dot_general(a, b, ((dims[0], dims[1]), ((), ())), preferred_element_type=F32)


NN = ((1,), (0,))
NT = ((1,), (1,))
TN = ((0,), (0,))


def spin(u, cosine, sine):
    width = u.shape[-1]
    times = width // cosine.shape[-1]
    cosine, sine = (jnp.concatenate([table] * times, axis=1) for table in (cosine, sine))
    lane = lax.broadcasted_iota(jnp.int32, u.shape, 1)
    other = jnp.where(
        lane % HEAD_DIM < HALF, pltpu.roll(u, width - HALF, 1), pltpu.roll(u, HALF, 1)
    )
    return u * cosine + other * sine


def head_mask(shape, head):
    lane = lax.broadcasted_iota(jnp.int32, shape, 1)
    return lane // HEAD_DIM == head


def attend_kernel(rows, n_t, place, own, *refs):
    lows, highs = refs[: n_t - 1], refs[n_t - 1 : 2 * n_t - 2]
    mine, other, cosine, sine, seg_col, seg_row = refs[2 * n_t - 2 : 2 * n_t + 4]
    q, k, v, ctx, lse, normed, w_qkv = refs[2 * n_t + 4 :]
    length, width = q.shape
    piece = own.shape[0]
    heads = width // HEAD_DIM
    block_rows = mine.shape[1]

    normed[:piece, :] = own[...]
    for by in range(1, n_t):
        there = slice(by * piece, (by + 1) * piece)

        @pl.when(place[0] + by < n_t)
        def _(there=there, by=by):
            normed[there, :] = highs[by - 1][...]

        @pl.when(place[0] + by >= n_t)
        def _(there=there, by=by):
            normed[there, :] = lows[n_t - by - 1][...]

    for m in range(mine.shape[0]):
        even = slice(2 * m * block_rows, (2 * m + 1) * block_rows)
        odd = slice((2 * m + 1) * block_rows, (2 * m + 2) * block_rows)

        @pl.when(place[1] == 0)
        def _(m=m, even=even, odd=odd):
            w_qkv[even, :] = mine[m]
            w_qkv[odd, :] = other[m]

        @pl.when(place[1] == 1)
        def _(m=m, even=even, odd=odd):
            w_qkv[even, :] = other[m]
            w_qkv[odd, :] = mine[m]

    @pl.loop(0, length // rows)
    def _(block):
        here = pl.ds(pl.multiple_of(block * rows, rows), rows)
        proj = dot(normed[here, :], w_qkv[...], NN)
        cos_here, sin_here = cosine[here, :], sine[here, :]
        q[here, :] = spin(proj[:, :width], cos_here, sin_here).astype(BF16)
        k[here, :] = spin(proj[:, width : 2 * width], cos_here, sin_here).astype(BF16)
        v[here, :] = proj[:, 2 * width :].astype(BF16)

    @pl.loop(0, length // rows)
    def _(block):
        here = pl.ds(pl.multiple_of(block * rows, rows), rows)
        q_here = q[here, :]
        same = seg_col[here, :] == seg_row[...]
        total = jnp.zeros((rows, width), F32)
        for head in range(heads):
            mine = head_mask((rows, width), head)
            q_head = jnp.where(mine, q_here, jnp.zeros_like(q_here)) * BF16(SCALE)
            scores = jnp.where(same, dot(q_head, k[...], NT), MASKED)
            highest = jnp.max(scores, axis=1, keepdims=True)
            weights = jnp.exp(scores - highest)
            sums = jnp.sum(weights, axis=1, keepdims=True)
            mixed = dot(weights.astype(BF16), v[...], NN) * (1.0 / sums)
            total = jnp.where(mine, mixed, total)
            lse[here, head : head + 1] = highest + jnp.log(sums)
        ctx[here, :] = total.astype(BF16)


def attend(place, lows, highs, mine, other, cosine, sine, seg_col, seg_row):
    length, width = cosine.shape[0], mine.shape[-1] // 3
    d_model = lows[0].shape[1]
    rows = min(ROWS, length)
    heads = width // HEAD_DIM
    cost = pl.CostEstimate(
        flops=2 * length * d_model * 3 * width + 4 * length * length * width * 4,
        bytes_accessed=8 * 2**20,
        transcendentals=heads * length * length,
    )
    wide = jax.ShapeDtypeStruct((length, width), BF16)
    whole = pl.BlockSpec()
    arrays = (*lows, *highs[1:], mine, other, cosine, sine, seg_col, seg_row)
    return pl.pallas_call(
        functools.partial(attend_kernel, rows, len(lows)),
        in_specs=[pl.BlockSpec(memory_space=pltpu.SMEM)] + [whole] * len(arrays),
        out_specs=[whole] * 7,
        out_shape=(
            wide,
            wide,
            wide,
            wide,
            jax.ShapeDtypeStruct((length, 128), F32),
            jax.ShapeDtypeStruct((length, d_model), BF16),
            jax.ShapeDtypeStruct((d_model, 3 * width), BF16),
        ),
        compiler_params=pltpu.CompilerParams(vmem_limit_bytes=48 * 2**20),
        cost_estimate=cost,
        name="attend",
    )(place, *arrays)


def attend_back_kernel(
    rows, dctx, q, k, v, lse_row, cosine, sine, seg_col, seg_row, dproj, dk_sum, dv_sum
):
    length, width = q.shape
    heads = width // HEAD_DIM
    dk_sum[...] = jnp.zeros_like(dk_sum)
    dv_sum[...] = jnp.zeros_like(dv_sum)

    @pl.loop(0, length // rows)
    def _(block):
        here = pl.ds(pl.multiple_of(block * rows, rows), rows)
        q_here, dctx_here = q[here, :], dctx[here, :]
        same = seg_col[...] == seg_row[:, here]
        dq = jnp.zeros((rows, width), F32)
        for head in range(heads):
            mine = head_mask((rows, width), head)
            q_head = jnp.where(mine, q_here, jnp.zeros_like(q_here)) * BF16(SCALE)
            dctx_head = jnp.where(mine, dctx_here, jnp.zeros_like(dctx_here))
            scores = jnp.where(same, dot(k[...], q_head, NT), MASKED)
            chances = jnp.exp(scores - lse_row[head : head + 1, here])
            grads = dot(v[...], dctx_head, NT)
            both = chances * grads
            inner = jnp.sum(both, axis=0, keepdims=True)
            dscores = (both - chances * inner).astype(BF16)
            dv_sum[...] += dot(chances.astype(BF16), dctx_head, NN)
            dk_sum[...] += dot(dscores, q_head, NN)
            dq = jnp.where(mine, dot(dscores, k[...], TN), dq)
        dq = spin(dq * SCALE, cosine[here, :], -sine[here, :])
        dproj[here, :width] = dq.astype(BF16)

    @pl.loop(0, length // rows)
    def _(block):
        here = pl.ds(pl.multiple_of(block * rows, rows), rows)
        dk = spin(dk_sum[here, :], cosine[here, :], -sine[here, :])
        dproj[here, width : 2 * width] = dk.astype(BF16)
        dproj[here, 2 * width :] = dv_sum[here, :].astype(BF16)


def attend_back(dctx, q, k, v, lse_row, cosine, sine, seg_col, seg_row):
    length, width = q.shape
    rows = min(ROWS, length)
    heads = width // HEAD_DIM
    cost = pl.CostEstimate(
        flops=10 * length * length * width * 4,
        bytes_accessed=8 * 2**20,
        transcendentals=heads * length * length,
    )
    return pl.pallas_call(
        functools.partial(attend_back_kernel, rows),
        out_shape=jax.ShapeDtypeStruct((length, 3 * width), BF16),
        scratch_shapes=[pltpu.VMEM((length, width), F32), pltpu.VMEM((length, width), F32)],
        compiler_params=pltpu.CompilerParams(vmem_limit_bytes=48 * 2**20),
        cost_estimate=cost,
        name="attend_back",
    )(dctx, q, k, v, lse_row, cosine, sine, seg_col, seg_row)


def normalize(rows):
    average = jnp.mean(rows, axis=-1, keepdims=True)
    centred = rows - average
    inv_std = lax.rsqrt(jnp.mean(centred * centred, axis=-1, keepdims=True) + EPSILON)
    return centred * inv_std, inv_std


def norm_back(grads, gain, scaled, inv_std):
    inner = grads * gain
    mean_grad = jnp.mean(inner, axis=-1, keepdims=True)
    mean_proj = jnp.mean(inner * scaled, axis=-1, keepdims=True)
    return inv_std * (inner - mean_grad - scaled * mean_proj)


def on_device(
    n_dp,
    n_t,
    block_in,
    segment_ids,
    norm1_gain,
    w_qkv,
    w_out,
    norm2_gain,
    w_in,
    w_mlp_out,
    out_grad,
):
    n_quad = n_dp // 2
    bits = [1 << b for b in range(n_quad.bit_length() - 1)]
    d_index, t_index = lax.axis_index("dp"), lax.axis_index("tensor")
    quad, first_core = d_index // 2, d_index % 2 == 0
    piece, d_model = block_in.shape[1], block_in.shape[2]
    length = piece * n_t
    width = w_qkv.shape[2]
    span = d_model // n_quad

    def core(x):
        return lax.ppermute(x, "dp", [(i, i ^ 1) for i in range(n_dp)])

    def pair(x, bit):
        return lax.ppermute(x, "dp", [(i, i ^ (2 * bit)) for i in range(n_dp)])

    def ahead(x, by):
        return lax.ppermute(x, "tensor", [(i, (i + by) % n_t) for i in range(n_t)])

    def across(x, mask):
        return lax.ppermute(x, "tensor", [(i, i ^ mask) for i in range(n_t)])

    def pick(a, b):
        return jnp.where(first_core, a, b)

    def reorder(x):
        cuts = [
            lax.dynamic_slice_in_dim(x, (quad ^ m) * span, span, axis=x.ndim - 1)
            for m in range(n_quad)
        ]
        return jnp.concatenate(cuts, axis=-1)

    def resume(side, values):
        with jax.named_scope(side["name"]):
            try:
                side["held"] = side["task"].send(values)
            except StopIteration as end:
                side.update(task=None, held=end.value)

    def begin(name, task):
        side = {"name": name, "task": task, "held": None}
        resume(side, None)
        return side

    def hold(chain, *sides):
        chain, held = lax.optimization_barrier((chain, [side["held"] for side in sides]))
        for side, values in zip(sides, held):
            side["held"] = values
        return chain

    def follow(chain, *sides):
        chain = hold(chain, *sides)
        for side in sides:
            if side["task"] is not None:
                resume(side, side["held"])
        return chain

    def wait_for(marker, values):
        return lax.optimization_barrier((marker, values))[1]

    def finish(side):
        while side["task"] is not None:
            resume(side, side["held"])
        return side["held"]

    def pair_turn(x, hop, flip=0):
        steps = [(bits[hop], bits[::-1][hop])[(i + flip) % 2] for i in range(n_dp)]
        return lax.ppermute(x, "dp", [(i, i ^ (2 * steps[i])) for i in range(n_dp)])

    def pair_gather(x, flip=0):
        held, labels = [x], [[0], [0]]
        orders = (bits[::-1], bits) if flip else (bits, bits[::-1])
        for hop in range(len(bits)):
            sent = yield pair_turn(jnp.stack(held), hop, flip)
            held = held + [sent[n] for n in range(len(held))]
            labels = [
                some + [m ^ order[hop] for m in some]
                for some, order in zip(labels, orders)
            ]
        places = [[some.index(m) for m in range(n_quad)] for some in labels]
        return [held[a] if a == b else pick(held[a], held[b]) for a, b in zip(*places)]

    def pair_scatter(blocks):
        held, labels = list(blocks), [list(range(n_quad))] * 2

        def chosen(wanted):
            spots = [[some.index(m) for m in want] for some, want in zip(labels, wanted)]
            return [held[a] if a == b else pick(held[a], held[b]) for a, b in zip(*spots)]

        for hop in range(len(bits)):
            turns = bits[hop], bits[::-1][hop]
            stays = [[m for m in some if not m & bit] for some, bit in zip(labels, turns)]
            goes = [[m | bit for m in some] for some, bit in zip(stays, turns)]
            sent, kept = yield pair_turn(jnp.stack(chosen(goes)), hop), chosen(stays)
            held = [
                (stay.astype(F32) + sent[n].astype(F32)).astype(BF16)
                for n, stay in enumerate(kept)
            ]
            labels = stays
        return held[0]

    def core_scatter(blocks):
        evens, odds = blocks[0::2], blocks[1::2]
        sent = core(jnp.stack([pick(b, a) for a, b in zip(evens, odds)]))
        kept = [pick(a, b) for a, b in zip(evens, odds)]
        sent, kept = yield sent, kept
        return [
            (stay.astype(F32) + sent[n].astype(F32)).astype(BF16) for n, stay in enumerate(kept)
        ]

    doublings = [1 << i for i in range(n_t.bit_length() - 1)]

    def line_swaps(x):
        held = [x]
        for mask in doublings:
            sent = yield across(jnp.stack(held), mask)
            held = held + [sent[n] for n in range(len(held))]
        return held

    def line_scatter(held):
        for mask in doublings[::-1]:
            sent, held = yield across(jnp.stack(held[mask:]), mask), held[:mask]
            held = [
                (stay.astype(F32) + sent[n].astype(F32)).astype(BF16)
                for n, stay in enumerate(held)
            ]
        return held[0]

    def to_line(held):
        held = jnp.stack(held)
        return [
            lax.dynamic_index_in_dim(held, t_index ^ ((t_index + s) % n_t), 0, False)
            for s in range(n_t)
        ]

    def from_line(held):
        return [
            lax.dynamic_index_in_dim(held, ((t_index ^ m) - t_index) % n_t, 0, False)
            for m in range(n_t)
        ]

    masks = list(range(0, n_t, 2))
    block = d_model // n_dp
    half = w_mlp_out.shape[0] // 2

    def qkv_weights(local):
        local = jnp.concatenate([local[0], local[1], local[2]], axis=1)
        mine = yield from pair_gather(local)
        mine = jnp.stack(mine)
        mine, other = yield mine, core(mine)
        return mine, other

    def out_rows(local, ids):
        ids = ids.astype(BF16).reshape(piece // block, block)
        tail = -ids.shape[0] % 16
        packed = jnp.concatenate([local, jnp.pad(ids, ((0, tail), (0, 0)))])
        return [packed] + [ahead(packed, -by) for by in range(1, n_t)]

    def out_weights(local):
        mine = yield from pair_gather(local, 1)
        mine = jnp.stack(mine)
        mine, other = yield mine, core(mine)
        first, second = pick(mine, other), pick(other, mine)
        return jnp.concatenate(
            [part for m in range(n_quad) for part in (first[m], second[m])], axis=1
        )

    def mlp_weights(local):
        even, odd = local[:, :half], local[:, half:]
        other = yield core(pick(odd, even))
        start = jnp.concatenate([pick(even, other), pick(other, odd)], axis=-1)
        blocks = yield from pair_gather(start)
        return jnp.concatenate(blocks, axis=-1)

    def mlp_gradients(tokens, dy_tokens, acts):
        dact, dgate, prod = acts
        grads = jnp.stack(
            [
                dot(dact, tokens, TN).astype(BF16),
                dot(dgate, tokens, TN).astype(BF16),
                dot(prod, dy_tokens, TN).astype(BF16),
            ]
        )
        total = yield from pair_scatter(
            [grads[:, :, m * span : (m + 1) * span] for m in range(n_quad)]
        )
        low, high = total[..., :block], total[..., block:]
        own, other = yield pick(low, high), core(pick(high, low))
        first, second = pick(own, other), pick(other, own)
        ends = [
            jnp.concatenate([part[:, n * half : (n + 1) * half] for part in (first, second)], axis=1)
            for n in range(len(masks))
        ]
        moved = yield ends[:1] + [across(end, mask) for mask, end in zip(masks[1:], ends[1:])]
        return sum(end.astype(F32) for end in moved)

    def mlp_output(near, far):
        both = yield core(jnp.stack([near[piece:].astype(BF16), far[piece:].astype(BF16)]))
        back = yield across((far[:piece] + both[1].astype(F32)).astype(BF16), 1)
        return both[0].astype(F32) + back.astype(F32)

    def out_gradients(rows, grads):
        partial = dot(rows, grads, TN).astype(BF16)
        cuts = [partial[:, i * block : (i + 1) * block] for i in range(n_dp)]
        parts = yield from core_scatter(cuts)
        low = yield from pair_scatter(parts)
        total = yield from line_scatter(from_line(low.reshape(n_t, width, block)))
        return total.astype(F32)

    def qkv_gradients(rows, grads):
        partial = dot(rows, grads, TN).astype(BF16)
        cuts = [partial[i * block : (i + 1) * block] for i in range(n_dp)]
        parts = yield from core_scatter(cuts)
        total = yield from pair_scatter(parts)
        return total.astype(F32)

    def gain_gradients(parts):
        total = reorder(parts)
        hops = [functools.partial(across, mask=mask) for mask in doublings] + [core]
        hops += [functools.partial(pair, bit=bit) for bit in bits]
        for hop in hops:
            total, other = yield total, hop(total)
            total = total + other
        return total

    x = reorder(block_in[0]).astype(F32)
    gain1, gain2 = reorder(norm1_gain), reorder(norm2_gain)
    scaled1, inv_std1 = normalize(x)
    own = (scaled1 * gain1).astype(BF16)
    with jax.named_scope("out_weights"):
        rows = out_rows(w_out, segment_ids)
    own, w_qkv, w_in, w_mlp_out, out_grad = wait_for(
        rows[1:], (own, w_qkv, w_in, w_mlp_out, out_grad)
    )
    ids = [part[width : width + piece // block].reshape(1, piece) for part in rows]
    segments = jnp.concatenate(ids, axis=1).astype(jnp.int32)
    out_local = jnp.concatenate([part[:width] for part in rows], axis=0)
    qkv_side = begin("qkv_weights", qkv_weights(w_qkv))
    mlp_local = jnp.stack([w_in[0].T, w_in[1].T, w_mlp_out])
    mlp_sides = [begin("mlp_weights", mlp_weights(mlp_local))]
    resume(mlp_sides[0], mlp_sides[0]["held"])
    low, high = [own], [own]
    for hop in range(1, n_t):
        ups = [(i, i + 1) for i in range(hop - 1, n_t - 1)]
        downs = [(n_t - 1 - i, n_t - 1 - j) for i, j in ups]
        with jax.named_scope("normed_gather"):
            low.append(lax.ppermute(low[-1], "tensor", ups))
            high.append(lax.ppermute(high[-1], "tensor", downs))
        if hop == 1:
            low[1], high[1], mlp_far = follow((low[1], high[1], mlp_local), qkv_side)
            with jax.named_scope("mlp_weights"):
                slices = [across(mlp_far, mask) for mask in masks[1:]]
            places = (t_index * piece + jnp.arange(length, dtype=jnp.int32)) % length
            firsts = jnp.sum((segments < segments.reshape(length, 1)).astype(jnp.int32), axis=1)
            lane = jnp.arange(2 * HEAD_DIM, dtype=jnp.int32)
            freqs = jnp.power(ROPE_BASE, -(lane % HALF).astype(F32) * 2.0 / HEAD_DIM)
            signs = jnp.where(lane % HEAD_DIM < HALF, -1.0, 1.0)
            angles = (places - firsts).astype(F32)[:, None] * freqs[None, :]
            cosine, sine = jnp.cos(angles), jnp.sin(angles) * signs[None, :]
            seg_col = segments.reshape(length, 1)
        elif hop == 2:
            low[2], high[2], cosine, sine, seg_col, out_local, out_grad = follow(
                hold(
                    (low[2], high[2], cosine, sine, seg_col, out_local, out_grad), mlp_sides[0]
                ),
                qkv_side,
            )
            out_side = begin("out_weights", out_weights(out_local))
        elif hop == 3:
            low[3], high[3], slices = follow(
                (low[3], high[3], slices), out_side, qkv_side, mlp_sides[0]
            )
            mlp_sides += [begin("mlp_weights", mlp_weights(local)) for local in slices]
    dy = reorder(out_grad[0])
    with jax.named_scope("dy_tokens"):
        dy_moves = core(dy), across(dy, 1)
    high[-1] = follow(high[-1], *mlp_sides[1:])

    place = jnp.stack([t_index, d_index % 2]).astype(jnp.int32)
    q, k, v, ctx_local, lse, normed, qkv_full = attend(
        place, low, high, *finish(qkv_side), cosine, sine, seg_col, segments
    )
    lse_row = lse[:, : max(8, width // HEAD_DIM)].T

    ctx_local, dy_moves = follow((ctx_local, dy_moves), out_side, *mlp_sides)
    with jax.named_scope("context"):
        ctx_pieces = [ahead(ctx_local[s * piece : (s + 1) * piece], s) for s in range(1, n_t)]
    ctx_pieces = [ctx_local[:piece]] + ctx_pieces
    ctx = jnp.concatenate([ctx_pieces[(n_t - s) % n_t] for s in range(n_t)], axis=1)
    out_full = finish(out_side)
    hidden = x + dot(ctx, out_full, NN)

    scaled2, inv_std2 = normalize(hidden)
    normed2 = (scaled2 * gain2).astype(BF16)
    with jax.named_scope("normed2_tokens"):
        n2_core, n2_far = core(normed2), across(normed2, 1)
    with jax.named_scope("dy_tokens"):
        dy_near = jnp.concatenate([dy, dy_moves[0]])
        dy_far = wait_for(n2_core, dy_moves[1])
        dy_far = jnp.concatenate([dy_far, core(dy_far)])
    with jax.named_scope("mlp_weights"):
        for side in mlp_sides[1:]:
            side["held"] = wait_for(n2_core, side["held"])
        up, gate_up, down = (
            jnp.concatenate(parts) for parts in zip(*[finish(side) for side in mlp_sides])
        )

    def mlp_tokens(rows, dy_rows):
        act, gate = dot(rows, up, NT), dot(rows, gate_up, NT)
        dprod = dot(dy_rows, down, NT)
        below = 0.5 * (1.0 + lax.erf(act * (0.5**0.5)))
        slope = below + act * jnp.exp(-0.5 * act * act) * 0.3989422804014327
        gelu = act * below
        prod = (gelu * gate).astype(BF16)
        dact = (dprod * gate * slope).astype(BF16)
        dgate = (dprod * gelu).astype(BF16)
        return (dact, dgate, prod), dot(dact, up, NN) + dot(dgate, gate_up, NN)

    n2_near = jnp.concatenate([normed2, n2_core])
    near_acts, dn2_near = mlp_tokens(n2_near, dy_near)
    n2_far, near_acts, dn2_near = lax.optimization_barrier((n2_far, near_acts, dn2_near))
    with jax.named_scope("normed2_tokens"):
        n2_far = jnp.concatenate([n2_far, core(n2_far)])
    far_acts, dn2_far = mlp_tokens(n2_far, dy_far)
    with jax.named_scope("dn2_tokens"):
        dn2_core = core(jnp.stack([dn2_near[piece:].astype(BF16), dn2_far[piece:].astype(BF16)]))
        dn2_send = (dn2_far[:piece] + dn2_core[1].astype(F32)).astype(BF16)
        dn2_send, near_acts, far_acts = lax.optimization_barrier((dn2_send, near_acts, far_acts))
        dn2_back = across(dn2_send, 1)
    grads_side = begin(
        "mlp_grads",
        mlp_gradients(
            jnp.concatenate([n2_near, n2_far]),
            jnp.concatenate([dy_near, dy_far]),
            [jnp.concatenate(both) for both in zip(near_acts, far_acts)],
        ),
    )
    with jax.named_scope("mlp_out"):
        mlp_near, mlp_far = dot(near_acts[2], down, NN), dot(far_acts[2], down, NN)
    mlp_side = begin("mlp_out", mlp_output(mlp_near, mlp_far))
    dn2_own = dn2_near[:piece] + dn2_core[0].astype(F32) + dn2_back.astype(F32)
    dh = dy.astype(F32) + norm_back(dn2_own, gain2, scaled2, inv_std2)
    gain2_part = jnp.sum(dn2_own * scaled2, axis=0)
    dh_low = dh.astype(BF16)

    dctx = dot(dh_low, out_full, NT).astype(BF16)
    with jax.named_scope("dctx"):
        dctx_pieces = [ahead(dctx[:, s * width : (s + 1) * width], s) for s in range(1, n_t)]

    out_side = begin("out_grads", out_gradients(ctx, dh_low))
    dctx_pieces = [dctx[:, :width]] + dctx_pieces
    dctx_local = jnp.concatenate([dctx_pieces[(n_t - s) % n_t] for s in range(n_t)], axis=0)
    dctx_local = follow(dctx_local, out_side, mlp_side)
    dproj = attend_back(dctx_local, q, k, v, lse_row, cosine, sine, seg_col, segments)
    dn1 = dot(dproj, qkv_full, NT)
    gain1_part = jnp.sum(dn1 * normed.astype(F32), axis=0) / gain1
    dn1_low = dn1.astype(BF16)
    cuts = [dn1_low[s * piece : (s + 1) * piece] for s in range(n_t)]
    with jax.named_scope("dn1_sum"):
        highs = lax.ppermute(cuts[n_t - 1], "tensor", [(0, 1)])
        lows = lax.ppermute(cuts[1], "tensor", [(n_t - 1, n_t - 2)])
    dproj = follow(dproj, grads_side, mlp_side, out_side)
    cuts, dproj, normed = lax.optimization_barrier((cuts, dproj, normed))
    gains_side = begin("gains", gain_gradients(jnp.stack([gain1_part, gain2_part])))
    for hop in range(2, n_t):
        if hop == 2:
            dproj, normed = wait_for(lows, (dproj, normed))
            lows, highs = follow((lows, highs), gains_side, out_side)
            qkv_side = begin("qkv_grads", qkv_gradients(normed, dproj))
            resume(qkv_side, qkv_side["held"])
        else:
            lows, highs = follow((lows, highs), grads_side, gains_side, out_side, qkv_side)
        with jax.named_scope("dn1_sum"):
            ups = [(i, i + 1) for i in range(hop)]
            downs = [(n_t - 1 - i, n_t - 1 - j) for i, j in ups]
            lows = (cuts[hop].astype(F32) + lows.astype(F32)).astype(BF16)
            highs = (cuts[n_t - hop].astype(F32) + highs.astype(F32)).astype(BF16)
            lows, highs = lax.ppermute(lows, "tensor", downs), lax.ppermute(highs, "tensor", ups)
        if hop == 2:
            cuts = follow(cuts, grads_side)
    lows, highs = follow((lows, highs), grads_side)
    dn1_own = cuts[0].astype(F32) + lows.astype(F32) + highs.astype(F32)
    in_grad = reorder(dh + norm_back(dn1_own, gain1, scaled1, inv_std1))
    block_out = reorder((hidden + mlp_near[:piece] + finish(mlp_side)).astype(BF16))

    gains = finish(gains_side)
    mlp_sum = finish(grads_side)
    qkv_sum = finish(qkv_side)
    w_qkv_grad = jnp.stack([qkv_sum[:, c * width : (c + 1) * width] for c in range(3)])
    return (
        block_out[None],
        in_grad[None],
        gains[0],
        w_qkv_grad,
        finish(out_side),
        gains[1],
        jnp.stack([mlp_sum[0].T, mlp_sum[1].T]),
        mlp_sum[2],
    )


def solution(mesh):
    in_specs = (
        P("dp", "tensor", None),
        P("dp", "tensor"),
        P(),
        P(None, "dp", "tensor"),
        P("tensor", "dp"),
        P(),
        P(None, "dp", "tensor"),
        P("tensor", "dp"),
        P("dp", "tensor", None),
    )
    out_specs = (
        P("dp", "tensor", None),
        P("dp", "tensor", None),
        P(),
        P(None, "dp", "tensor"),
        P("tensor", "dp"),
        P(),
        P(None, "dp", "tensor"),
        P("tensor", "dp"),
    )
    return jax.shard_map(
        functools.partial(on_device, mesh.shape["dp"], mesh.shape["tensor"]),
        mesh=mesh,
        in_specs=in_specs,
        out_specs=out_specs,
        check_vma=False,
    )
```

```python
import functools

import jax
import jax.numpy as jnp
from jax import lax
from jax.experimental import pallas as pl
from jax.experimental.pallas import tpu as pltpu
from jax.sharding import PartitionSpec as P

HEAD_DIM = 64
HALF = HEAD_DIM // 2
EPSILON = 1e-05
ROPE_BASE = 160000.0
MASKED = -1e30
ROWS = 1024
SCALE = HEAD_DIM ** (-0.5)
F32 = jnp.float32
BF16 = jnp.bfloat16


def dot(a, b, dims):
    return lax.dot_general(a, b, ((dims[0], dims[1]), ((), ())), preferred_element_type=F32)


NN = ((1,), (0,))
NT = ((1,), (1,))
TN = ((0,), (0,))


def spin(u, cosine, sine):
    width = u.shape[-1]
    times = width // cosine.shape[-1]
    cosine, sine = (jnp.concatenate([table] * times, axis=1) for table in (cosine, sine))
    lane = lax.broadcasted_iota(jnp.int32, u.shape, 1)
    other = jnp.where(
        lane % HEAD_DIM < HALF, pltpu.roll(u, width - HALF, 1), pltpu.roll(u, HALF, 1)
    )
    return u * cosine + other * sine


def head_mask(shape, head):
    lane = lax.broadcasted_iota(jnp.int32, shape, 1)
    return lane // HEAD_DIM == head


def attend_kernel(rows, n_t, place, own, *refs):
    lows, highs = refs[: n_t - 1], refs[n_t - 1 : 2 * n_t - 2]
    mine, other, cosine, sine, seg_col, seg_row = refs[2 * n_t - 2 : 2 * n_t + 4]
    q, k, v, ctx, lse, normed, w_qkv = refs[2 * n_t + 4 :]
    length, width = q.shape
    piece = own.shape[0]
    heads = width // HEAD_DIM
    block_rows = mine.shape[1]

    normed[:piece, :] = own[...]
    for by in range(1, n_t):
        there = slice(by * piece, (by + 1) * piece)

        @pl.when(place[0] + by < n_t)
        def _(there=there, by=by):
            normed[there, :] = highs[by - 1][...]

        @pl.when(place[0] + by >= n_t)
        def _(there=there, by=by):
            normed[there, :] = lows[n_t - by - 1][...]

    for m in range(mine.shape[0]):
        even = slice(2 * m * block_rows, (2 * m + 1) * block_rows)
        odd = slice((2 * m + 1) * block_rows, (2 * m + 2) * block_rows)

        @pl.when(place[1] == 0)
        def _(m=m, even=even, odd=odd):
            w_qkv[even, :] = mine[m]
            w_qkv[odd, :] = other[m]

        @pl.when(place[1] == 1)
        def _(m=m, even=even, odd=odd):
            w_qkv[even, :] = other[m]
            w_qkv[odd, :] = mine[m]

    @pl.loop(0, length // rows)
    def _(block):
        here = pl.ds(pl.multiple_of(block * rows, rows), rows)
        proj = dot(normed[here, :], w_qkv[...], NN)
        cos_here, sin_here = cosine[here, :], sine[here, :]
        q[here, :] = spin(proj[:, :width], cos_here, sin_here).astype(BF16)
        k[here, :] = spin(proj[:, width : 2 * width], cos_here, sin_here).astype(BF16)
        v[here, :] = proj[:, 2 * width :].astype(BF16)

    @pl.loop(0, length // rows)
    def _(block):
        here = pl.ds(pl.multiple_of(block * rows, rows), rows)
        q_here = q[here, :]
        same = seg_col[here, :] == seg_row[...]
        total = jnp.zeros((rows, width), F32)
        for head in range(heads):
            mine = head_mask((rows, width), head)
            q_head = jnp.where(mine, q_here, jnp.zeros_like(q_here)) * BF16(SCALE)
            scores = jnp.where(same, dot(q_head, k[...], NT), MASKED)
            highest = jnp.max(scores, axis=1, keepdims=True)
            weights = jnp.exp(scores - highest)
            sums = jnp.sum(weights, axis=1, keepdims=True)
            mixed = dot(weights.astype(BF16), v[...], NN) * (1.0 / sums)
            total = jnp.where(mine, mixed, total)
            lse[here, head : head + 1] = highest + jnp.log(sums)
        ctx[here, :] = total.astype(BF16)


def attend(place, lows, highs, mine, other, cosine, sine, seg_col, seg_row):
    length, width = cosine.shape[0], mine.shape[-1] // 3
    d_model = lows[0].shape[1]
    rows = min(ROWS, length)
    heads = width // HEAD_DIM
    cost = pl.CostEstimate(
        flops=2 * length * d_model * 3 * width + 4 * length * length * width * 4,
        bytes_accessed=8 * 2**20,
        transcendentals=heads * length * length,
    )
    wide = jax.ShapeDtypeStruct((length, width), BF16)
    whole = pl.BlockSpec()
    arrays = (*lows, *highs[1:], mine, other, cosine, sine, seg_col, seg_row)
    return pl.pallas_call(
        functools.partial(attend_kernel, rows, len(lows)),
        in_specs=[pl.BlockSpec(memory_space=pltpu.SMEM)] + [whole] * len(arrays),
        out_specs=[whole] * 7,
        out_shape=(
            wide,
            wide,
            wide,
            wide,
            jax.ShapeDtypeStruct((length, 128), F32),
            jax.ShapeDtypeStruct((length, d_model), BF16),
            jax.ShapeDtypeStruct((d_model, 3 * width), BF16),
        ),
        compiler_params=pltpu.CompilerParams(vmem_limit_bytes=48 * 2**20),
        cost_estimate=cost,
        name="attend",
    )(place, *arrays)


def attend_back_kernel(
    rows, dctx, q, k, v, lse_row, cosine, sine, seg_col, seg_row, dproj, dk_sum, dv_sum
):
    length, width = q.shape
    heads = width // HEAD_DIM
    single = rows == length
    if not single:
        dk_sum[...] = jnp.zeros_like(dk_sum)
        dv_sum[...] = jnp.zeros_like(dv_sum)

    @pl.loop(0, length // rows)
    def _(block):
        here = pl.ds(pl.multiple_of(block * rows, rows), rows)
        q_here, dctx_here = q[here, :], dctx[here, :]
        same = seg_col[...] == seg_row[:, here]
        dq = jnp.zeros((rows, width), F32)
        for head in range(heads):
            mine = head_mask((rows, width), head)
            q_head = jnp.where(mine, q_here, jnp.zeros_like(q_here)) * BF16(SCALE)
            dctx_head = jnp.where(mine, dctx_here, jnp.zeros_like(dctx_here))
            scores = jnp.where(same, dot(k[...], q_head, NT), MASKED)
            chances = jnp.exp(scores - lse_row[head : head + 1, here])
            grads = dot(v[...], dctx_head, NT)
            both = chances * grads
            inner = jnp.sum(both, axis=0, keepdims=True)
            dscores = (both - chances * inner).astype(BF16)
            dv_part = dot(chances.astype(BF16), dctx_head, NN)
            dk_part = dot(dscores, q_head, NN)
            if single and head == 0:
                dv_sum[...] = dv_part
                dk_sum[...] = dk_part
            else:
                dv_sum[...] += dv_part
                dk_sum[...] += dk_part
            dq = jnp.where(mine, dot(dscores, k[...], TN), dq)
        dq = spin(dq * SCALE, cosine[here, :], -sine[here, :])
        dproj[here, :width] = dq.astype(BF16)

    @pl.loop(0, length // rows)
    def _(block):
        here = pl.ds(pl.multiple_of(block * rows, rows), rows)
        dk = spin(dk_sum[here, :], cosine[here, :], -sine[here, :])
        dproj[here, width : 2 * width] = dk.astype(BF16)
        dproj[here, 2 * width :] = dv_sum[here, :].astype(BF16)


def attend_back(dctx, q, k, v, lse_row, cosine, sine, seg_col, seg_row):
    length, width = q.shape
    rows = min(ROWS, length)
    heads = width // HEAD_DIM
    cost = pl.CostEstimate(
        flops=10 * length * length * width * 4,
        bytes_accessed=8 * 2**20,
        transcendentals=heads * length * length,
    )
    return pl.pallas_call(
        functools.partial(attend_back_kernel, rows),
        out_shape=jax.ShapeDtypeStruct((length, 3 * width), BF16),
        scratch_shapes=[pltpu.VMEM((length, width), F32), pltpu.VMEM((length, width), F32)],
        compiler_params=pltpu.CompilerParams(vmem_limit_bytes=48 * 2**20),
        cost_estimate=cost,
        name="attend_back",
    )(dctx, q, k, v, lse_row, cosine, sine, seg_col, seg_row)


def normalize(rows):
    average = jnp.mean(rows, axis=-1, keepdims=True)
    centred = rows - average
    inv_std = lax.rsqrt(jnp.mean(centred * centred, axis=-1, keepdims=True) + EPSILON)
    return centred * inv_std, inv_std


def norm_back(grads, gain, scaled, inv_std):
    inner = grads * gain
    mean_grad = jnp.mean(inner, axis=-1, keepdims=True)
    mean_proj = jnp.mean(inner * scaled, axis=-1, keepdims=True)
    return inv_std * (inner - mean_grad - scaled * mean_proj)


def on_device(
    n_dp,
    n_t,
    block_in,
    segment_ids,
    norm1_gain,
    w_qkv,
    w_out,
    norm2_gain,
    w_in,
    w_mlp_out,
    out_grad,
):
    n_quad = n_dp // 2
    bits = [1 << b for b in range(n_quad.bit_length() - 1)]
    d_index, t_index = lax.axis_index("dp"), lax.axis_index("tensor")
    quad, first_core = d_index // 2, d_index % 2 == 0
    piece, d_model = block_in.shape[1], block_in.shape[2]
    length = piece * n_t
    width = w_qkv.shape[2]
    span = d_model // n_quad

    def core(x):
        return lax.ppermute(x, "dp", [(i, i ^ 1) for i in range(n_dp)])

    def pair(x, bit):
        return lax.ppermute(x, "dp", [(i, i ^ (2 * bit)) for i in range(n_dp)])

    def ahead(x, by):
        return lax.ppermute(x, "tensor", [(i, (i + by) % n_t) for i in range(n_t)])

    def across(x, mask):
        return lax.ppermute(x, "tensor", [(i, i ^ mask) for i in range(n_t)])

    def pick(a, b):
        return jnp.where(first_core, a, b)

    def reorder(x):
        cuts = [
            lax.dynamic_slice_in_dim(x, (quad ^ m) * span, span, axis=x.ndim - 1)
            for m in range(n_quad)
        ]
        return jnp.concatenate(cuts, axis=-1)

    def resume(side, values):
        with jax.named_scope(side["name"]):
            try:
                side["held"] = side["task"].send(values)
            except StopIteration as end:
                side.update(task=None, held=end.value)

    def begin(name, task):
        side = {"name": name, "task": task, "held": None}
        resume(side, None)
        return side

    def hold(chain, *sides):
        chain, held = lax.optimization_barrier((chain, [side["held"] for side in sides]))
        for side, values in zip(sides, held):
            side["held"] = values
        return chain

    def follow(chain, *sides):
        chain = hold(chain, *sides)
        for side in sides:
            if side["task"] is not None:
                resume(side, side["held"])
        return chain

    def wait_for(marker, values):
        return lax.optimization_barrier((marker, values))[1]

    def finish(side):
        while side["task"] is not None:
            resume(side, side["held"])
        return side["held"]

    def pair_turn(x, hop, flip=0):
        steps = [(bits[hop], bits[::-1][hop])[(i + flip) % 2] for i in range(n_dp)]
        return lax.ppermute(x, "dp", [(i, i ^ (2 * steps[i])) for i in range(n_dp)])

    def pair_gather(x, flip=0):
        held, labels = [x], [[0], [0]]
        orders = (bits[::-1], bits) if flip else (bits, bits[::-1])
        for hop in range(len(bits)):
            sent = yield pair_turn(jnp.stack(held), hop, flip)
            held = held + [sent[n] for n in range(len(held))]
            labels = [
                some + [m ^ order[hop] for m in some]
                for some, order in zip(labels, orders)
            ]
        places = [[some.index(m) for m in range(n_quad)] for some in labels]
        return [held[a] if a == b else pick(held[a], held[b]) for a, b in zip(*places)]

    def pair_scatter(blocks):
        held, labels = list(blocks), [list(range(n_quad))] * 2

        def chosen(wanted):
            spots = [[some.index(m) for m in want] for some, want in zip(labels, wanted)]
            return [held[a] if a == b else pick(held[a], held[b]) for a, b in zip(*spots)]

        for hop in range(len(bits)):
            turns = bits[hop], bits[::-1][hop]
            stays = [[m for m in some if not m & bit] for some, bit in zip(labels, turns)]
            goes = [[m | bit for m in some] for some, bit in zip(stays, turns)]
            sent, kept = yield pair_turn(jnp.stack(chosen(goes)), hop), chosen(stays)
            held = [
                (stay.astype(F32) + sent[n].astype(F32)).astype(BF16)
                for n, stay in enumerate(kept)
            ]
            labels = stays
        return held[0]

    def core_scatter(blocks):
        evens, odds = blocks[0::2], blocks[1::2]
        sent = core(jnp.stack([pick(b, a) for a, b in zip(evens, odds)]))
        kept = [pick(a, b) for a, b in zip(evens, odds)]
        sent, kept = yield sent, kept
        return [
            (stay.astype(F32) + sent[n].astype(F32)).astype(BF16) for n, stay in enumerate(kept)
        ]

    doublings = [1 << i for i in range(n_t.bit_length() - 1)]

    def line_swaps(x):
        held = [x]
        for mask in doublings:
            sent = yield across(jnp.stack(held), mask)
            held = held + [sent[n] for n in range(len(held))]
        return held

    def line_scatter(held):
        for mask in doublings[::-1]:
            sent, held = yield across(jnp.stack(held[mask:]), mask), held[:mask]
            held = [
                (stay.astype(F32) + sent[n].astype(F32)).astype(BF16)
                for n, stay in enumerate(held)
            ]
        return held[0]

    def to_line(held):
        held = jnp.stack(held)
        return [
            lax.dynamic_index_in_dim(held, t_index ^ ((t_index + s) % n_t), 0, False)
            for s in range(n_t)
        ]

    def from_line(held):
        return [
            lax.dynamic_index_in_dim(held, ((t_index ^ m) - t_index) % n_t, 0, False)
            for m in range(n_t)
        ]

    masks = list(range(0, n_t, 2))
    block = d_model // n_dp
    half = w_mlp_out.shape[0] // 2

    def qkv_weights(local):
        local = jnp.concatenate([local[0], local[1], local[2]], axis=1)
        mine = yield from pair_gather(local)
        mine = jnp.stack(mine)
        mine, other = yield mine, core(mine)
        return mine, other

    def out_rows(local, ids):
        ids = ids.astype(BF16).reshape(piece // block, block)
        tail = -ids.shape[0] % 16
        packed = jnp.concatenate([local, jnp.pad(ids, ((0, tail), (0, 0)))])
        return [packed] + [ahead(packed, -by) for by in range(1, n_t)]

    def out_weights(local):
        mine = yield from pair_gather(local, 1)
        mine = jnp.stack(mine)
        mine, other = yield mine, core(mine)
        first, second = pick(mine, other), pick(other, mine)
        return jnp.concatenate(
            [part for m in range(n_quad) for part in (first[m], second[m])], axis=1
        )

    def mlp_weights(local):
        even, odd = local[:, :half], local[:, half:]
        other = yield core(pick(odd, even))
        start = jnp.concatenate([pick(even, other), pick(other, odd)], axis=-1)
        blocks = yield from pair_gather(start)
        return jnp.concatenate(blocks, axis=-1)

    def mlp_gradients(tokens, dy_tokens, acts):
        dact, dgate, prod = acts
        grads = jnp.stack(
            [
                dot(dact, tokens, TN).astype(BF16),
                dot(dgate, tokens, TN).astype(BF16),
                dot(prod, dy_tokens, TN).astype(BF16),
            ]
        )
        total = yield from pair_scatter(
            [grads[:, :, m * span : (m + 1) * span] for m in range(n_quad)]
        )
        low, high = total[..., :block], total[..., block:]
        own, other = yield pick(low, high), core(pick(high, low))
        first, second = pick(own, other), pick(other, own)
        ends = [
            jnp.concatenate([part[:, n * half : (n + 1) * half] for part in (first, second)], axis=1)
            for n in range(len(masks))
        ]
        moved = yield ends[:1] + [across(end, mask) for mask, end in zip(masks[1:], ends[1:])]
        return sum(end.astype(F32) for end in moved)

    def mlp_output(near, far):
        both = yield core(jnp.stack([near[piece:].astype(BF16), far[piece:].astype(BF16)]))
        back = yield across((far[:piece] + both[1].astype(F32)).astype(BF16), 1)
        return both[0].astype(F32) + back.astype(F32)

    def out_gradients(rows, grads):
        partial = dot(rows, grads, TN).astype(BF16)
        cuts = [partial[:, i * block : (i + 1) * block] for i in range(n_dp)]
        parts = yield from core_scatter(cuts)
        low = yield from pair_scatter(parts)
        total = yield from line_scatter(from_line(low.reshape(n_t, width, block)))
        return total.astype(F32)

    def qkv_gradients(rows, grads):
        partial = dot(rows, grads, TN).astype(BF16)
        cuts = [partial[i * block : (i + 1) * block] for i in range(n_dp)]
        parts = yield from core_scatter(cuts)
        total = yield from pair_scatter(parts)
        return total.astype(F32)

    def gain_gradients(parts):
        total = reorder(parts)
        hops = [functools.partial(across, mask=mask) for mask in doublings] + [core]
        hops += [functools.partial(pair, bit=bit) for bit in bits]
        for hop in hops:
            total, other = yield total, hop(total)
            total = total + other
        return total

    x = reorder(block_in[0]).astype(F32)
    gain1, gain2 = reorder(norm1_gain), reorder(norm2_gain)
    scaled1, inv_std1 = normalize(x)
    own = (scaled1 * gain1).astype(BF16)
    with jax.named_scope("out_weights"):
        rows = out_rows(w_out, segment_ids)
    own, w_qkv, w_in, w_mlp_out, out_grad = wait_for(
        rows[1:], (own, w_qkv, w_in, w_mlp_out, out_grad)
    )
    ids = [part[width : width + piece // block].reshape(1, piece) for part in rows]
    segments = jnp.concatenate(ids, axis=1).astype(jnp.int32)
    out_local = jnp.concatenate([part[:width] for part in rows], axis=0)
    qkv_side = begin("qkv_weights", qkv_weights(w_qkv))
    mlp_local = jnp.stack([w_in[0].T, w_in[1].T, w_mlp_out])
    mlp_sides = [begin("mlp_weights", mlp_weights(mlp_local))]
    resume(mlp_sides[0], mlp_sides[0]["held"])
    low, high = [own], [own]
    for hop in range(1, n_t):
        ups = [(i, i + 1) for i in range(hop - 1, n_t - 1)]
        downs = [(n_t - 1 - i, n_t - 1 - j) for i, j in ups]
        with jax.named_scope("normed_gather"):
            low.append(lax.ppermute(low[-1], "tensor", ups))
            high.append(lax.ppermute(high[-1], "tensor", downs))
        if hop == 1:
            low[1], high[1], mlp_far = follow((low[1], high[1], mlp_local), qkv_side)
            with jax.named_scope("mlp_weights"):
                slices = [across(mlp_far, mask) for mask in masks[1:]]
            places = (t_index * piece + jnp.arange(length, dtype=jnp.int32)) % length
            firsts = jnp.sum((segments < segments.reshape(length, 1)).astype(jnp.int32), axis=1)
            lane = jnp.arange(2 * HEAD_DIM, dtype=jnp.int32)
            freqs = jnp.power(ROPE_BASE, -(lane % HALF).astype(F32) * 2.0 / HEAD_DIM)
            signs = jnp.where(lane % HEAD_DIM < HALF, -1.0, 1.0)
            angles = (places - firsts).astype(F32)[:, None] * freqs[None, :]
            cosine, sine = jnp.cos(angles), jnp.sin(angles) * signs[None, :]
            seg_col = segments.reshape(length, 1)
        elif hop == 2:
            low[2], high[2], cosine, sine, seg_col, out_local, out_grad = follow(
                hold(
                    (low[2], high[2], cosine, sine, seg_col, out_local, out_grad), mlp_sides[0]
                ),
                qkv_side,
            )
            out_side = begin("out_weights", out_weights(out_local))
        elif hop == 3:
            low[3], high[3], slices = follow(
                (low[3], high[3], slices), out_side, qkv_side, mlp_sides[0]
            )
            mlp_sides += [begin("mlp_weights", mlp_weights(local)) for local in slices]
    dy = reorder(out_grad[0])
    with jax.named_scope("dy_tokens"):
        dy_moves = core(dy), across(dy, 1)
    high[-1] = follow(high[-1], *mlp_sides[1:])

    place = jnp.stack([t_index, d_index % 2]).astype(jnp.int32)
    q, k, v, ctx_local, lse, normed, qkv_full = attend(
        place, low, high, *finish(qkv_side), cosine, sine, seg_col, segments
    )
    lse_row = lse[:, : max(8, width // HEAD_DIM)].T

    ctx_local, dy_moves = follow((ctx_local, dy_moves), out_side, *mlp_sides)
    with jax.named_scope("context"):
        ctx_pieces = [ahead(ctx_local[s * piece : (s + 1) * piece], s) for s in range(1, n_t)]
    ctx_pieces = [ctx_local[:piece]] + ctx_pieces
    ctx = jnp.concatenate([ctx_pieces[(n_t - s) % n_t] for s in range(n_t)], axis=1)
    out_full = finish(out_side)
    hidden = x + dot(ctx, out_full, NN)

    scaled2, inv_std2 = normalize(hidden)
    normed2 = (scaled2 * gain2).astype(BF16)
    with jax.named_scope("normed2_tokens"):
        n2_core, n2_far = core(normed2), across(normed2, 1)
    with jax.named_scope("dy_tokens"):
        dy_near = jnp.concatenate([dy, dy_moves[0]])
        dy_far = wait_for(n2_core, dy_moves[1])
        dy_far = jnp.concatenate([dy_far, core(dy_far)])
    with jax.named_scope("mlp_weights"):
        for side in mlp_sides[1:]:
            side["held"] = wait_for(n2_core, side["held"])
        up, gate_up, down = (
            jnp.concatenate(parts) for parts in zip(*[finish(side) for side in mlp_sides])
        )

    def mlp_tokens(rows, dy_rows):
        act, gate = dot(rows, up, NT), dot(rows, gate_up, NT)
        dprod = dot(dy_rows, down, NT)
        below = 0.5 * (1.0 + lax.erf(act * (0.5**0.5)))
        slope = below + act * jnp.exp(-0.5 * act * act) * 0.3989422804014327
        gelu = act * below
        prod = (gelu * gate).astype(BF16)
        dact = (dprod * gate * slope).astype(BF16)
        dgate = (dprod * gelu).astype(BF16)
        return (dact, dgate, prod), dot(dact, up, NN) + dot(dgate, gate_up, NN)

    n2_near = jnp.concatenate([normed2, n2_core])
    near_acts, dn2_near = mlp_tokens(n2_near, dy_near)
    n2_far, near_acts, dn2_near = lax.optimization_barrier((n2_far, near_acts, dn2_near))
    with jax.named_scope("normed2_tokens"):
        n2_far = jnp.concatenate([n2_far, core(n2_far)])
    far_acts, dn2_far = mlp_tokens(n2_far, dy_far)
    with jax.named_scope("dn2_tokens"):
        dn2_core = core(jnp.stack([dn2_near[piece:].astype(BF16), dn2_far[piece:].astype(BF16)]))
        dn2_send = (dn2_far[:piece] + dn2_core[1].astype(F32)).astype(BF16)
        dn2_send, near_acts, far_acts = lax.optimization_barrier((dn2_send, near_acts, far_acts))
        dn2_back = across(dn2_send, 1)
    grads_side = begin(
        "mlp_grads",
        mlp_gradients(
            jnp.concatenate([n2_near, n2_far]),
            jnp.concatenate([dy_near, dy_far]),
            [jnp.concatenate(both) for both in zip(near_acts, far_acts)],
        ),
    )
    with jax.named_scope("mlp_out"):
        mlp_near, mlp_far = dot(near_acts[2], down, NN), dot(far_acts[2], down, NN)
    mlp_side = begin("mlp_out", mlp_output(mlp_near, mlp_far))
    dn2_own = dn2_near[:piece] + dn2_core[0].astype(F32) + dn2_back.astype(F32)
    dh = dy.astype(F32) + norm_back(dn2_own, gain2, scaled2, inv_std2)
    gain2_part = jnp.sum(dn2_own * scaled2, axis=0)
    dh_low = dh.astype(BF16)

    dctx = dot(dh_low, out_full, NT).astype(BF16)
    with jax.named_scope("dctx"):
        dctx_pieces = [ahead(dctx[:, s * width : (s + 1) * width], s) for s in range(1, n_t)]

    out_side = begin("out_grads", out_gradients(ctx, dh_low))
    dctx_pieces = [dctx[:, :width]] + dctx_pieces
    dctx_local = jnp.concatenate([dctx_pieces[(n_t - s) % n_t] for s in range(n_t)], axis=0)
    dctx_local = follow(dctx_local, out_side, mlp_side)
    dproj = attend_back(dctx_local, q, k, v, lse_row, cosine, sine, seg_col, segments)
    dn1 = dot(dproj, qkv_full, NT)
    gain1_part = jnp.sum(dn1 * normed.astype(F32), axis=0) / gain1
    dn1_low = dn1.astype(BF16)
    cuts = [dn1_low[s * piece : (s + 1) * piece] for s in range(n_t)]
    with jax.named_scope("dn1_sum"):
        highs = lax.ppermute(cuts[n_t - 1], "tensor", [(0, 1)])
        lows = lax.ppermute(cuts[1], "tensor", [(n_t - 1, n_t - 2)])
    dproj = follow(dproj, grads_side, mlp_side, out_side)
    cuts, dproj, normed = lax.optimization_barrier((cuts, dproj, normed))
    gains_side = begin("gains", gain_gradients(jnp.stack([gain1_part, gain2_part])))
    for hop in range(2, n_t):
        if hop == 2:
            dproj, normed = wait_for(lows, (dproj, normed))
            lows, highs = follow((lows, highs), gains_side, out_side)
            qkv_side = begin("qkv_grads", qkv_gradients(normed, dproj))
            resume(qkv_side, qkv_side["held"])
        else:
            lows, highs = follow((lows, highs), grads_side, gains_side, out_side, qkv_side)
        with jax.named_scope("dn1_sum"):
            ups = [(i, i + 1) for i in range(hop)]
            downs = [(n_t - 1 - i, n_t - 1 - j) for i, j in ups]
            lows = (cuts[hop].astype(F32) + lows.astype(F32)).astype(BF16)
            highs = (cuts[n_t - hop].astype(F32) + highs.astype(F32)).astype(BF16)
            lows, highs = lax.ppermute(lows, "tensor", downs), lax.ppermute(highs, "tensor", ups)
        if hop == 2:
            cuts = follow(cuts, grads_side)
    lows, highs = follow((lows, highs), grads_side)
    dn1_own = cuts[0].astype(F32) + lows.astype(F32) + highs.astype(F32)
    in_grad = reorder(dh + norm_back(dn1_own, gain1, scaled1, inv_std1))
    block_out = reorder((hidden + mlp_near[:piece] + finish(mlp_side)).astype(BF16))

    gains = finish(gains_side)
    mlp_sum = finish(grads_side)
    qkv_sum = finish(qkv_side)
    w_qkv_grad = jnp.stack([qkv_sum[:, c * width : (c + 1) * width] for c in range(3)])
    return (
        block_out[None],
        in_grad[None],
        gains[0],
        w_qkv_grad,
        finish(out_side),
        gains[1],
        jnp.stack([mlp_sum[0].T, mlp_sum[1].T]),
        mlp_sum[2],
    )


def solution(mesh):
    in_specs = (
        P("dp", "tensor", None),
        P("dp", "tensor"),
        P(),
        P(None, "dp", "tensor"),
        P("tensor", "dp"),
        P(),
        P(None, "dp", "tensor"),
        P("tensor", "dp"),
        P("dp", "tensor", None),
    )
    out_specs = (
        P("dp", "tensor", None),
        P("dp", "tensor", None),
        P(),
        P(None, "dp", "tensor"),
        P("tensor", "dp"),
        P(),
        P(None, "dp", "tensor"),
        P("tensor", "dp"),
    )
    return jax.shard_map(
        functools.partial(on_device, mesh.shape["dp"], mesh.shape["tensor"]),
        mesh=mesh,
        in_specs=in_specs,
        out_specs=out_specs,
        check_vma=False,
    )
```
